32 devices in a mesh: dp: 8 (over y, x, core), blk: 4 (over z).
Axes of the slice: x: 2, y: 2, z: 4, core: 2. Of those that a mesh axis runs over, the one named last changes fastest.
Arguments:
- inputs: bfloat16 [32, 256, 768], P('dp', 'blk'), may hold values from -6 to 6
- teacher: bfloat16 [32, 256, 768], P('dp', 'blk'), may hold values from -9 to 9
- counts: int32 [8], P('dp'), may hold values from 2 to 4, as said below
- groups: int32 [32], P('dp'), may hold values from 0 to 7
- group_weight: float32 [8], replicated, may hold values from 0.5 to 2
- w_qkv: float32 [768, 2304], P(None, 'dp'), may hold values from -0.3125 to 0.3125
- w_out: float32 [768, 768], P(None, 'dp'), may hold values from -0.875 to 0.875
- w_fc: float32 [768, 3072], P(None, 'dp'), may hold values from -0.21875 to 0.21875
- w_proj: float32 [3072, 768], P('dp'), may hold values from -0.15625 to 0.15625
- vectors: float32 [12, 768], replicated, as said below
- mom_qkv: float32 [768, 2304], P(None, 'dp'), as said below
- mom_out: float32 [768, 768], P(None, 'dp'), as said below
- mom_fc: float32 [768, 3072], P(None, 'dp'), as said below
- mom_proj: float32 [3072, 768], P('dp'), as said below
Outputs:
- outputs: bfloat16 [32, 256, 768], P('dp', 'blk')
- input_grad: float32 [32, 256, 768], P('dp', 'blk')
- mom_qkv_new: float32 [768, 2304], P(None, 'dp')
- mom_out_new: float32 [768, 768], P(None, 'dp')
- mom_fc_new: float32 [768, 3072], P(None, 'dp')
- mom_proj_new: float32 [3072, 768], P('dp')
- qkv_new: float32 [768, 2304], P(None, 'dp')
- out_new: float32 [768, 768], P(None, 'dp')
- fc_new: float32 [768, 3072], P(None, 'dp')
- proj_new: float32 [3072, 768], P('dp')
- qkv_copy: bfloat16 [768, 2304], P(None, 'dp')
- out_copy: bfloat16 [768, 768], P(None, 'dp')
- fc_copy: bfloat16 [768, 3072], P(None, 'dp')
- proj_copy: bfloat16 [3072, 768], P('dp')
- vec_grad_total: float32 [12, 768], replicated
- vectors_new: float32 [12, 768], replicated
The draws below stay inside these ranges and needn't reach their ends.
Inputs may be any that keep to these rules, and one draw needn't show every extreme that they name: Entry d counts the sequences of dp index d that enter the loss: its first so many slots; some entry equals 4. `vectors`: rows 0 and 5 are gains near 1, rows 1 and 6 shifts, rows 2, 3, 4 the query, value and attention-output biases, the next 4 rows the feed-forward bias, the last the projection bias. `mom_qkv`: of both signs, no structure. `mom_out`: of both signs, no structure. `mom_fc`: of both signs, no structure. `mom_proj`: of both signs, no structure.
All inputs are finite; a program needn't handle non-finite values.
Results may differ from the reference program's by a relative error of at most 0.018.
Values may be sent and summed in bfloat16 or wider, within the bound.
A program may use at most 192 MiB of HBM per device.

```python
import math
import jax
import jax.numpy as jnp
from jax import lax

D = 768
H = 12
HD = 64
QKV = 2304
FF = 3072
GROUPS = 8
ITERS = 5
SLOTS = 4
SEQ_LEN = 256
SEQS = 32
DP_RANKS = 8
VROWS = 12


def draw_counts(key, part):
    key = jax.random.fold_in(key, 1)
    first_key, second_key = jax.random.split(key)
    base_counts = jax.random.randint(first_key, (DP_RANKS,), SLOTS // 2, SLOTS + 1)
    full_index = jax.random.randint(second_key, (), 0, DP_RANKS)
    return jnp.where(jnp.arange(DP_RANKS) == full_index, SLOTS, base_counts).astype(jnp.int32)


def moment_like(key, shape):
    spread = 0.5 * math.sqrt(SEQS * SEQ_LEN)
    return (spread * jax.random.truncated_normal(key, -4.0, 4.0, shape, jnp.float32)).astype(jnp.float32)


def draw_mom_qkv(key, part):
    key = jax.random.fold_in(key, 2)
    return moment_like(key, (D, QKV))


def draw_mom_out(key, part):
    key = jax.random.fold_in(key, 3)
    return moment_like(key, (D, D))


def draw_mom_fc(key, part):
    key = jax.random.fold_in(key, 4)
    return moment_like(key, (D, FF))


def draw_mom_proj(key, part):
    key = jax.random.fold_in(key, 5)
    return moment_like(key, (FF, D))


def draw_vectors(key, part):
    key = jax.random.fold_in(key, 7)
    first_key, second_key = jax.random.split(key)
    uniform_part = jax.random.uniform(first_key, (VROWS, D), jnp.float32, -1.0, 1.0)
    normal_part = jax.random.truncated_normal(second_key, -4.0, 4.0, (VROWS, D), jnp.float32)
    row_ids = jnp.arange(VROWS)[:, None]
    is_gain = (row_ids == 0) | (row_ids == 5)
    return jnp.where(is_gain, 1.0 + 0.3 * uniform_part, 0.4 * normal_part).astype(jnp.float32)


def plant(array, own_key, low, largest):
    index_at = [jax.random.randint(jax.random.fold_in(own_key, axis), (), 0, length) for axis, length in enumerate(array.shape)]
    widest = array.shape.index(max(array.shape))
    neighbour = index_at[:widest] + [(index_at[widest] + 1) % array.shape[widest]] + index_at[widest + 1:]
    return array.at[tuple(index_at)].set(low).at[tuple(neighbour)].set(largest)


def block_scale(key, extent, pieces, low, high):
    gain = 1.0
    for dim, blocks in pieces:
        draws = jax.random.uniform(jax.random.fold_in(jax.random.fold_in(key, 6), dim), (blocks,), jnp.float32, low / len(pieces), high / len(pieces))
        gain = gain * jnp.repeat(jnp.exp(draws), extent[dim] // blocks).reshape((-1,) + (1,) * (len(extent) - 1 - dim))
    return gain


def scatter_about(stream_key, shape, scale, reach, pieces=(), kind=jnp.bfloat16):
    entries = scale * jax.random.normal(stream_key, shape, jnp.float32)
    if pieces:
        entries = entries * block_scale(stream_key, shape, pieces, -0.22, 0.18)
    return jnp.clip(entries, -reach, reach).astype(kind)


def setup_inputs(seed: int = 0) -> dict:
    key_list = jax.random.split(jax.random.key(seed), 15)
    inputs = scatter_about(key_list[0], (SEQS, SEQ_LEN, D), 1.0, 6.0, ((0, 8), (1, 4)))
    teacher = scatter_about(key_list[1], (SEQS, SEQ_LEN, D), 1.5, 9.0, ((0, 8), (1, 4)))
    counts = draw_counts(jax.random.fold_in(key_list[14], 71), 0)
    groups = plant(jax.random.randint(key_list[3], (SEQS,), 0, GROUPS), jax.random.fold_in(key_list[3], 1), 0, GROUPS - 1).astype(jnp.int32)
    group_weight = jnp.clip(jnp.exp(jax.random.uniform(key_list[4], (GROUPS,), jnp.float32, math.log(0.5), math.log(2.0))), 0.5, 2.0)
    w_qkv = scatter_about(key_list[5], (D, QKV), (D // 2) ** -0.5, 0.3125, ((1, 8),), jnp.float32)
    w_out = scatter_about(key_list[6], (D, D), (D // 16) ** -0.5, 0.875, ((1, 8),), jnp.float32)
    w_fc = scatter_about(key_list[7], (D, FF), D ** -0.5, 0.21875, ((1, 8),), jnp.float32)
    w_proj = scatter_about(key_list[8], (FF, D), (FF // 2) ** -0.5, 0.15625, ((0, 8),), jnp.float32)
    vectors = draw_vectors(jax.random.fold_in(key_list[14], 71), 0)
    mom_qkv = draw_mom_qkv(jax.random.fold_in(key_list[14], 71), 0)
    mom_out = draw_mom_out(jax.random.fold_in(key_list[14], 71), 0)
    mom_fc = draw_mom_fc(jax.random.fold_in(key_list[14], 71), 0)
    mom_proj = draw_mom_proj(jax.random.fold_in(key_list[14], 71), 0)
    return dict(inputs=inputs, teacher=teacher, counts=counts, groups=groups, group_weight=group_weight, w_qkv=w_qkv, w_out=w_out, w_fc=w_fc, w_proj=w_proj, vectors=vectors, mom_qkv=mom_qkv, mom_out=mom_out, mom_fc=mom_fc, mom_proj=mom_proj)


@jax.custom_vjp
def low(v):
    return lax.optimization_barrier(v.astype(jnp.bfloat16)).astype(jnp.float32)

@jax.custom_vjp
def low_back(v):
    return v

def low_keep(v):
    return (low(v), None)

def low_pass(kept, grad):
    return (grad,)

def back_keep(v):
    return (v, None)

def back_low(kept, grad):
    return (low(grad),)
low.defvjp(low_keep, low_pass)
low_back.defvjp(back_keep, back_low)
NORM_EPS = 1e-05
TEMPER = 2.0
MOMENT_DECAY = 0.5
POLY_FIRST = 3.4445
POLY_SECOND = -4.775
POLY_THIRD = 2.0315
RATE_QKV = 1.0
RATE_OUT = 3.0
RATE_FC = 0.5
RATE_PROJ = 0.5
RATE_VEC = 0.3
MASKED = -1e+30
HIGHEST = lax.Precision.HIGHEST

def layer_norm(values, gain_row, bias_row):
    row_mean = lax.optimization_barrier(jnp.mean(values, axis=-1, keepdims=True))
    centered = values - row_mean
    row_var = lax.optimization_barrier(jnp.mean(centered * centered, axis=-1, keepdims=True))
    return centered * lax.rsqrt(row_var + NORM_EPS) * gain_row + bias_row

def attend(queries, keys_all, values_all):
    length = queries.shape[1]
    block_rows = 512 if length % 512 == 0 else length
    block_count = length // block_rows
    key_pos = jnp.arange(length, dtype=jnp.int32)

    def one_block(block_index):
        row_start = (block_index * block_rows).astype(jnp.int32)
        query_rows = lax.dynamic_slice_in_dim(queries, row_start, block_rows, 1)
        scores = jnp.einsum('gqhd,gkhd->ghqk', query_rows, keys_all, precision=HIGHEST) * 0.125
        scores = low_back(scores)
        query_pos = row_start + jnp.arange(block_rows, dtype=jnp.int32)
        visible = key_pos[None, :] <= query_pos[:, None]
        scores = jnp.where(visible, scores, MASKED)
        row_peak = lax.optimization_barrier(jnp.max(scores, axis=-1, keepdims=True))
        weights = jnp.exp(scores - row_peak)
        probs_low = low(weights / lax.optimization_barrier(jnp.sum(weights, axis=-1, keepdims=True)))
        return jnp.einsum('ghqk,gkhd->gqhd', probs_low, values_all, precision=HIGHEST)
    blocks = lax.map(jax.checkpoint(one_block), jnp.arange(block_count, dtype=jnp.int32))
    return jnp.moveaxis(blocks, 0, 1).reshape(queries.shape)

def group_forward(params, inputs_group, teacher_group, weight_group):
    w_qkv, w_out, w_fc, w_proj, vectors = params
    fc_rows = FF // D
    fc_bias = vectors[7:7 + fc_rows].reshape(FF)
    proj_bias = vectors[7 + fc_rows]
    qkv_low = low(w_qkv)
    out_low = low(w_out)
    fc_low = low(w_fc)
    proj_low = low(w_proj)
    normed = low(layer_norm(inputs_group, vectors[0], vectors[1]))
    mixed_qkv = jnp.einsum('gld,de->gle', normed, qkv_low, precision=HIGHEST)
    queries = low_back(low(mixed_qkv[..., :D] + vectors[2]))
    keys_all = low_back(low(mixed_qkv[..., D:2 * D]))
    values_all = low_back(low(mixed_qkv[..., 2 * D:] + vectors[3]))
    heads_shape = inputs_group.shape[:2] + (H, HD)
    attended = attend(queries.reshape(heads_shape), keys_all.reshape(heads_shape), values_all.reshape(heads_shape))
    attended = low_back(low(attended.reshape(inputs_group.shape)))
    hidden = inputs_group + low_back(jnp.einsum('gld,de->gle', attended, out_low, precision=HIGHEST)) + vectors[4]
    normed_two = low(layer_norm(hidden, vectors[5], vectors[6]))
    gate_in = low_back(jnp.einsum('gld,df->glf', normed_two, fc_low, precision=HIGHEST) + fc_bias)
    active = low(jax.nn.gelu(gate_in, approximate=True))
    outputs = hidden + low_back(jnp.einsum('glf,fd->gld', active, proj_low, precision=HIGHEST)) + proj_bias
    student = jax.nn.log_softmax(outputs / TEMPER, axis=-1)
    target = jax.nn.log_softmax(teacher_group / TEMPER, axis=-1)
    diverge = lax.optimization_barrier(jnp.sum(jnp.exp(target) * (target - student), axis=-1))
    loss_value = D * jnp.sum(weight_group[:, None] * diverge)
    return (loss_value, outputs)

def orthogonalize(matrix):
    scaled = matrix / (jnp.sqrt(jnp.sum(matrix * matrix)) + 1e-07)
    for sweep_index in range(ITERS):
        gram_matrix = jnp.dot(scaled, scaled.T, precision=HIGHEST)
        poly_term = POLY_SECOND * gram_matrix + POLY_THIRD * jnp.dot(gram_matrix, gram_matrix, precision=HIGHEST)
        scaled = POLY_FIRST * scaled + jnp.dot(poly_term, scaled, precision=HIGHEST)
    return scaled

def reference(inputs, teacher, counts, groups, group_weight, w_qkv, w_out, w_fc, w_proj, vectors, mom_qkv, mom_out, mom_fc, mom_proj):
    seq_ids = jnp.arange(SEQS, dtype=jnp.int32)
    counted = (seq_ids % SLOTS < counts[seq_ids // SLOTS]).astype(group_weight.dtype)
    seq_weight = group_weight[groups] * counted
    batches = SEQS // SLOTS
    shaped = inputs.astype(jnp.float32).reshape(batches, SLOTS, SEQ_LEN, D)
    teacher_all = teacher.astype(jnp.float32).reshape(batches, SLOTS, SEQ_LEN, D)
    weight_split = seq_weight.reshape(batches, SLOTS)

    def loss_of(params, inputs_all):

        def scan_step(running, scan_item):
            inputs_group, teacher_group, weight_group = scan_item
            loss_value, outputs = jax.checkpoint(group_forward)(params, inputs_group, teacher_group, weight_group)
            return (running + loss_value, outputs)
        summed, outputs = lax.scan(scan_step, jnp.zeros((), inputs_all.dtype), (inputs_all, teacher_all, weight_split))
        return (summed, outputs)
    params = (w_qkv, w_out, w_fc, w_proj, vectors)
    loss_value, backward, outputs = jax.vjp(loss_of, params, shaped, has_aux=True)
    gradients, input_grad = backward(jnp.ones((), loss_value.dtype))
    grad_qkv, grad_out, grad_fc, grad_proj, grad_vec = gradients
    mom_qkv_new = MOMENT_DECAY * mom_qkv + grad_qkv
    mom_out_new = MOMENT_DECAY * mom_out + grad_out
    mom_fc_new = MOMENT_DECAY * mom_fc + grad_fc
    mom_proj_new = MOMENT_DECAY * mom_proj + grad_proj
    qkv_new = w_qkv - RATE_QKV * math.sqrt(QKV / D) * orthogonalize(mom_qkv_new)
    out_new = w_out - RATE_OUT * orthogonalize(mom_out_new)
    fc_new = w_fc - RATE_FC * math.sqrt(FF / D) * orthogonalize(mom_fc_new)
    proj_new = w_proj - RATE_PROJ * math.sqrt(FF / D) * orthogonalize(mom_proj_new.T).T
    vectors_new = vectors - RATE_VEC * grad_vec * lax.rsqrt(lax.optimization_barrier(jnp.mean(grad_vec * grad_vec, axis=-1, keepdims=True)) + NORM_EPS)
    return (outputs.reshape(SEQS, SEQ_LEN, D).astype(jnp.bfloat16), input_grad.reshape(SEQS, SEQ_LEN, D), mom_qkv_new, mom_out_new, mom_fc_new, mom_proj_new, qkv_new, out_new, fc_new, proj_new, qkv_new.astype(jnp.bfloat16), out_new.astype(jnp.bfloat16), fc_new.astype(jnp.bfloat16), proj_new.astype(jnp.bfloat16), grad_vec, vectors_new)
```

```python
import functools
import math

import jax
import jax.numpy as jnp
from jax import lax
from jax.experimental import pallas as pl
from jax.experimental.pallas import tpu as pltpu
from jax.sharding import PartitionSpec as P

D = 768
H = 12
HD = 64
QKV = 2304
FF = 3072
GROUPS = 8
ITERS = 5

NORM_EPS = 1e-05
TEMPER = 2.0
MOMENT_DECAY = 0.5
POLY_FIRST = 3.4445
POLY_SECOND = -4.775
POLY_THIRD = 2.0315
RATE_QKV = 1.0
RATE_OUT = 3.0
RATE_FC = 0.5
RATE_PROJ = 0.5
RATE_VEC = 0.3
MASKED = -1e30
GELU_SCALE = math.sqrt(2.0 / math.pi)
f32 = jnp.float32
bf16 = jnp.bfloat16
HIGHEST = lax.Precision.HIGHEST


def dot_nn(a, b):
    return lax.dot_general(a, b, (((1,), (0,)), ((), ())), preferred_element_type=f32)


def dot_nt(a, b):
    return lax.dot_general(a, b, (((1,), (1,)), ((), ())), preferred_element_type=f32)


def dot_tn(a, b):
    return lax.dot_general(a, b, (((0,), (0,)), ((), ())), preferred_element_type=f32)


def norm_parts(values):
    row_mean = jnp.mean(values, axis=-1, keepdims=True)
    centered = values - row_mean
    row_var = jnp.mean(centered * centered, axis=-1, keepdims=True)
    scale = lax.rsqrt(row_var + NORM_EPS)
    return centered * scale, scale


def norm_back(unit, scale, gain, grad):
    grad_unit = grad * gain
    mean_one = jnp.mean(grad_unit, axis=-1, keepdims=True)
    mean_two = jnp.mean(grad_unit * unit, axis=-1, keepdims=True)
    grad_values = scale * (grad_unit - mean_one - unit * mean_two)
    return grad_values, jnp.sum(grad * unit, axis=0), jnp.sum(grad, axis=0)


def gelu_both(values):
    cubic = GELU_SCALE * (values + 0.044715 * values * values * values)
    tanh = jnp.tanh(cubic)
    half = 0.5 * (1.0 + tanh)
    slope = half + 0.5 * values * (1.0 - tanh * tanh) * GELU_SCALE * (
        1.0 + 3.0 * 0.044715 * values * values
    )
    return values * half, slope


def split_low(values):
    upper = lax.reduce_precision(values, 8, 7)
    return upper.astype(bf16), (values - upper).astype(bf16)


def three_pass(dot, a, b):
    a_up, a_low = split_low(a)
    b_up, b_low = split_low(b)
    return dot(a_up, b_up) + (dot(a_up, b_low) + dot(a_low, b_up))


def product(a, b, exact):
    if exact:
        return three_pass(dot_nn, a, b)
    return dot_nn(a.astype(bf16), b.astype(bf16))


def newton_schulz(rows, gram):
    norm = jnp.sqrt(jnp.trace(gram)) + 1e-07
    rows = rows / norm
    gram = gram / (norm * norm)
    for sweep in range(ITERS):
        exact = sweep in (0, 3, 4)
        square = product(gram, gram, exact)
        poly = POLY_SECOND * gram + POLY_THIRD * square
        rows = POLY_FIRST * rows + product(rows, poly, True)
        if sweep < ITERS - 1:
            half = POLY_FIRST * gram + product(poly, gram, exact)
            gram = POLY_FIRST * half + product(half, poly, exact)
    return rows


MESH = pl.DeviceIdType.MESH
VMEM_SPEC = pl.BlockSpec(memory_space=pltpu.VMEM)
ANY_SPEC = pl.BlockSpec(memory_space=pl.ANY)
HBM_SPEC = pl.BlockSpec(memory_space=pltpu.HBM)
SMEM_SPEC = pl.BlockSpec(memory_space=pltpu.SMEM)
VMEM_BYTES = 60 * 1024 * 1024
VMEM_MUON = 40 * 1024 * 1024
VMEM_FINISH = 36 * 1024 * 1024
ROWS = 16


def place():
    dp = lax.axis_index("dp")
    core = lax.rem(dp, 2)
    chip = lax.div(dp, 2)
    px = lax.rem(chip, 2)
    py = lax.div(chip, 2)
    return dp, core, chip, dp + 1 - 2 * core, dp + 2 - 4 * px, dp + 4 - 8 * py


def push(src, dst, send_sem, recv_sem, target):
    return pltpu.make_async_remote_copy(
        src_ref=src, dst_ref=dst, send_sem=send_sem, recv_sem=recv_sem,
        device_id=target, device_id_type=MESH,
    )


def greet(targets):
    barrier = pltpu.get_barrier_semaphore()
    for target in targets:
        pl.semaphore_signal(barrier, inc=1, device_id=target, device_id_type=MESH)
    pl.semaphore_wait(barrier, len(targets))


def row_splits(row):
    parts = []
    for _ in range(3):
        part = row.astype(bf16)
        parts.append(part.astype(f32))
        row = row - part.astype(f32)
    return jnp.concatenate(parts + [jnp.zeros((5, row.shape[1]), f32)], axis=0).astype(bf16)


def row_repeat(row):
    return jnp.broadcast_to(row, (8, row.shape[1])).astype(bf16)


class PairGather:
    def __init__(self, buf, send, recv, base, near):
        half = buf.shape[1] // 2
        self.copies = {}
        for part in range(2):
            rows = pl.ds(part * half, half)
            for side in range(2):
                index = base + 2 * part + side
                self.copies[side, part] = push(
                    buf.at[0, rows], buf.at[1 + side, rows], send.at[index], recv.at[index],
                    {"dp": near[side]},
                )

    def start(self, part):
        for side in range(2):
            self.copies[side, part].start()

    def wait(self, side, part):
        self.copies[side, part].wait_recv()

    def finish(self):
        for copy in self.copies.values():
            copy.wait_send()


class PairScatter:
    def __init__(self, part, inbox, send, recv, base, near):
        self.half = part.shape[1] // 2
        self.part, self.inbox = part, inbox
        self.copies = {}
        for half in range(2):
            rows = pl.ds(half * self.half, self.half)
            for side in range(2):
                index = base + 2 * half + side
                self.copies[side, half] = push(
                    part.at[side, rows], inbox.at[side, rows], send.at[index], recv.at[index],
                    {"dp": near[side]},
                )

    def put(self, side, half, values):
        self.part[side, pl.ds(half * self.half, self.half)] = values.astype(self.part.dtype)
        self.copies[side, half].start()

    def collect(self, half):
        rows = pl.ds(half * self.half, self.half)
        for side in range(2):
            self.copies[side, half].wait_recv()
        return self.inbox[0, rows].astype(f32) + self.inbox[1, rows].astype(f32)

    def finish(self):
        for copy in self.copies.values():
            copy.wait_send()


class PlaneScatter:
    def __init__(self, part, inbox, send, recv, base, xn, yn):
        self.count = part.shape[0] // 4
        self.half = self.count // 2
        self.part, self.inbox = part, inbox

        def copy(index, source, low, target):
            return push(
                part.at[self.rows(source, low)], inbox.at[index], send.at[base + index],
                recv.at[base + index], {"dp": target},
            )

        self.x_top, self.y_low = copy(0, 1, 0, xn), copy(1, 2, 1, yn)
        self.y_top, self.x_low = copy(2, 2, 0, yn), copy(3, 1, 1, xn)
        self.to_x, self.to_y = copy(4, 3, 0, xn), copy(5, 3, 1, yn)

    def rows(self, slot, low):
        return pl.ds(slot * self.count + low * self.half, self.half)

    def put(self, slot, values):
        self.part[pl.ds(slot * self.count, self.count)] = values.astype(self.part.dtype)
        if slot == 1:
            self.x_top.start()
        elif slot == 2:
            self.y_low.start()
        elif slot == 3:
            self.to_x.start()
            self.to_y.start()

    def add(self, rows, index):
        self.part[rows] = (
            self.part[rows].astype(f32) + self.inbox[index].astype(f32)
        ).astype(self.part.dtype)

    def relay(self):
        self.to_x.wait_recv()
        self.add(self.rows(2, 0), 4)
        self.y_top.start()
        self.to_y.wait_recv()
        self.add(self.rows(1, 1), 5)
        self.x_low.start()

    def collect(self):
        for copy in (self.x_top, self.y_low, self.y_top, self.x_low):
            copy.wait_recv()
        upper = self.inbox[0].astype(f32) + self.inbox[2].astype(f32)
        lower = self.inbox[3].astype(f32) + self.inbox[1].astype(f32)
        own = self.part[pl.ds(0, self.count)].astype(f32)
        return own + jnp.concatenate([upper, lower], axis=0)

    def finish(self):
        for copy in (self.x_top, self.y_low, self.y_top, self.x_low, self.to_x, self.to_y):
            copy.wait_send()


def softmax_half(values):
    values = values * (1.0 / TEMPER)
    shifted = jnp.exp(values - jnp.max(values, axis=-1, keepdims=True))
    return shifted / jnp.sum(shifted, axis=-1, keepdims=True)


class Sems:
    def __init__(self):
        self.used = 0

    def __call__(self, count):
        start = self.used
        self.used += count
        return start


class ShardGather:
    def __init__(self, buf, count, send, recv, sems, peers, sib):
        half = count // 2
        base = sems(6)
        base_sib = sems(4)
        dp, xn, yn, diag = peers
        self.recv_sib = []

        def rows(owner, part):
            start = owner * count + (half if part == 1 else 0)
            return pl.ds(pl.multiple_of(start, 16), count if part == 2 else half)

        def copy(index, owner, part, target):
            area = buf.at[rows(owner, part)]
            return push(area, area, send.at[index], recv.at[index], {"dp": target})

        self.out = [
            copy(base, dp, 0, xn), copy(base + 1, dp, 1, yn),
            copy(base + 2, dp, 1, xn), copy(base + 3, dp, 0, yn),
        ]
        self.into = [
            copy(base, xn, 0, xn), copy(base + 1, yn, 1, yn),
            copy(base + 2, xn, 1, xn), copy(base + 3, yn, 0, yn),
        ]
        self.on = [copy(base + 4, xn, 0, yn), copy(base + 5, yn, 1, xn)]
        self.on_into = [copy(base + 4, diag, 0, yn), copy(base + 5, diag, 1, xn)]
        self.over = [copy(base_sib + i, owner, 2, sib) for i, owner in enumerate(peers)]
        self.over_into = [
            copy(base_sib + i, owner + sib - dp, 2, sib) for i, owner in enumerate(peers)
        ]

    def start(self):
        for item in self.out:
            item.start()
        self.over[0].start()

    def relay(self):
        self.into[0].wait_recv()
        self.on[0].start()
        self.into[1].wait_recv()
        self.on[1].start()

    def cross(self):
        self.into[2].wait_recv()
        self.over[1].start()
        self.into[3].wait_recv()
        self.over[2].start()
        self.on_into[0].wait_recv()
        self.on_into[1].wait_recv()
        self.over[3].start()

    def arrive(self):
        for item in self.over_into:
            item.wait_recv()

    def finish(self):
        for item in self.out + self.on + self.over:
            item.wait_send()


def token_kernel(
    sizes,
    counts_ref, groups_ref, weight_ref, inputs_ref, teacher_ref, w_qkv_ref, w_out_ref,
    w_fc_ref, w_proj_ref, vec_ref,
    out_back_ref, grad_ref, sums_ref, total_ref, centers_ref,
    x_all, teacher_all, full_qkv, full_out, normed, qkv, probs, attended, att_low,
    fc_sets, proj_sets, wide_buf, tokens, active, slope, grad_y_all,
    grad_gate, part_ffn, inbox_ffn, means, fc_grads, proj_grads,
    swap_ffn, ffn_from, ffn_sum, chain_in, att_grad, grad_mixed, qkv_grads, out_grads, swap_att,
    inbox_att, att_sum, plane_in, rows_own, rows_in, rows_plane, load_sems, send, recv,
):
    width = vec_ref.shape[1]
    blocks, positions = inputs_ref.shape[:2]
    length = blocks * positions
    units = w_proj_ref.shape[0]
    n_qkv, n_out = w_qkv_ref.shape[0], w_out_ref.shape[0]
    dp, core, chip, sib, xn, yn = place()
    diag = xn + yn - dp
    peers = (dp, xn, yn, diag)
    z = lax.axis_index("blk")
    planes = lax.axis_size("blk")
    ranks = lax.axis_size("dp")
    root = z == 0
    near = (jnp.where(core == 0, yn, xn), jnp.where(core == 0, xn, yn))
    weight_near = near[1]
    near_chips = tuple(lax.div(item, 2) for item in near)
    to_sib = {"dp": sib}
    sems = Sems()

    def turn(k):
        return lax.rem(dp + k, ranks)

    def plane(k):
        return lax.rem(z + k, planes)

    def total(values):
        return jnp.sum(values, axis=0, keepdims=True)

    sharers = (
        [(0, {"dp": dp, "blk": plane(k)}) for k in range(1, planes)]
        + [(1, {"dp": sib, "blk": plane(k)}) for k in range(planes)]
        + [(2, {"dp": weight_near, "blk": plane(k)}) for k in range(planes)]
        + [(3, {"dp": weight_near + sib - dp, "blk": plane(k)}) for k in range(planes)]
    )
    far = [item for item in (near[0], near[0] + sib - dp, diag, diag + sib - dp)]
    greet([target for _, target in sharers] + [{"dp": item} for item in far])
    hidden_buf, grad_y = wide_buf.at[pl.ds(0, length)], wide_buf.at[pl.ds(length, length)]
    fc_load = pltpu.make_async_copy(
        w_fc_ref, slope.at[pl.ds(0, w_fc_ref.shape[0])], load_sems.at[0]
    )
    proj_load = pltpu.make_async_copy(w_proj_ref, wide_buf.at[pl.ds(0, units)], load_sems.at[1])
    fc_load.start()
    proj_load.start()

    full_qkv[pl.ds(pl.multiple_of(dp * n_qkv, 16), n_qkv)] = w_qkv_ref[...].astype(bf16)
    gather_qkv = ShardGather(full_qkv, n_qkv, send, recv, sems, peers, sib)
    gather_qkv.start()

    def token_exchange(source, target):
        at = sems(8)
        sends, waits = [], []
        for k in range(1, planes):
            other = plane(k)
            sends.append(
                push(
                    source.at[other], target.at[z], send.at[at + k], recv.at[at + z],
                    {"blk": other},
                )
            )
            waits.append(
                push(
                    source.at[other], target.at[other], send.at[at + k], recv.at[at + other],
                    {"blk": other},
                )
            )
        return sends, waits

    inputs_out, inputs_in = token_exchange(inputs_ref, x_all)
    teacher_out, teacher_in = token_exchange(teacher_ref, teacher_all)
    for copy in inputs_out:
        copy.start()
    x_all[z] = inputs_ref[z]
    full_out[pl.ds(pl.multiple_of(dp * n_out, 16), n_out)] = w_out_ref[...].astype(bf16)
    gather_out = ShardGather(full_out, n_out, send, recv, sems, peers, sib)
    fc_load.wait()
    proj_load.wait()
    fc_sets[0, 0] = slope[: w_fc_ref.shape[0]].astype(bf16).T
    proj_sets[0, 0] = wide_buf[:units].astype(bf16)
    at = sems(6)

    def weight_push(ref, source, goal, index, target):
        return push(ref.at[source], ref.at[goal], send.at[index], recv.at[index], {"dp": target})

    weights_sib, weights_near, weights_on = [
        [
            weight_push(ref, source, goal, at + 2 * i + j, target)
            for j, ref in enumerate((fc_sets, proj_sets))
        ]
        for i, (source, goal, target) in enumerate(
            (((0, 0), (1, 0), sib), ((0, 0), (0, 1), weight_near), ((0, 1), (1, 1), sib))
        )
    ]
    for copy in weights_sib + teacher_out:
        copy.start()
    teacher_all[z] = teacher_ref[z]

    gather_qkv.relay()
    gather_out.start()
    for copy in inputs_in:
        copy.wait_recv()
    x = x_all[...].reshape(length, width).astype(f32)
    unit_one, _ = norm_parts(x)
    center_one = vec_ref[1:2].astype(bf16).astype(f32)
    low_normed = (unit_one * vec_ref[0:1] + vec_ref[1:2]).astype(bf16)
    normed[...] = (unit_one * vec_ref[0:1] + (vec_ref[1:2] - center_one)).astype(bf16)
    gather_qkv.cross()
    gather_out.relay()
    for copy in weights_near:
        copy.start()
    gather_qkv.arrive()

    for part, bias in ((0, vec_ref[2:3]), (1, None), (2, vec_ref[3:4])):
        values = dot_nt(low_normed, full_qkv[part * width : (part + 1) * width])
        qkv[part] = (values if bias is None else values + bias).astype(bf16)
    center_out = (
        dot_nt(row_repeat(center_one), full_qkv[2 * width :])[0:1] + vec_ref[3:4]
    ).astype(bf16).astype(f32)

    pair_width = 2 * HD
    pair_count = H // 2
    lane = lax.broadcasted_iota(jnp.int32, (length, pair_width), 1)
    sides = (lane < HD, lane >= HD)
    visible = lax.broadcasted_iota(jnp.int32, (length, length), 1) <= lax.broadcasted_iota(
        jnp.int32, (length, length), 0
    )

    def only(values, side):
        return jnp.where(sides[side], values, jnp.zeros_like(values))

    @pl.loop(0, pair_count, unroll=3)
    def _(pair):
        lanes = pl.ds(pl.multiple_of(pair * pair_width, pair_width), pair_width)
        queries, keys, values = qkv[0, :, lanes], qkv[1, :, lanes], qkv[2, :, lanes]
        both = []
        for side in range(2):
            scores = dot_nt(only(queries, side), keys) * 0.125
            scores = jnp.where(visible, scores, MASKED)
            weights = jnp.exp(scores - jnp.max(scores, axis=-1, keepdims=True))
            weights = weights * (1.0 / jnp.sum(weights, axis=-1, keepdims=True))
            probs[2 * pair + side] = weights
            both.append(dot_nn(weights.astype(bf16), values))
        result = jnp.where(sides[0], both[0], both[1])
        attended[:, lanes] = result
        att_low[:, lanes] = result.astype(bf16)

    gather_out.cross()
    gather_out.arrive()
    hidden = x + dot_nt(att_low[...], full_out[...]) + vec_ref[4:5]
    hidden_buf[...] = hidden
    att_low[...] = (attended[...] - center_out).astype(bf16)

    gather = PairGather(tokens, send, recv, sems(4), near)
    half = length // 2
    for part in range(2):
        unit_two, _ = norm_parts(hidden[part * half : (part + 1) * half])
        tokens[0, pl.ds(part * half, half)] = (
            unit_two * vec_ref[5:6] + vec_ref[6:7]
        ).astype(bf16)
        gather.start(part)
    for copy in weights_near:
        copy.wait_recv()
    for copy in weights_on:
        copy.start()

    def by_core(row):
        low_row, high_row = row[:, :units], row[:, units:]
        return (
            jnp.where(core == 0, low_row, high_row), jnp.where(core == 0, high_row, low_row)
        )

    def bias_of(item):
        return by_core(vec_ref[pl.ds(7 + item, 1), :])

    own_bias = bias_of(chip)
    bias = (
        (own_bias[0], bias_of(near_chips[1])[0]), (own_bias[1], bias_of(near_chips[0])[1])
    )
    pieces = [(side, part) for part in range(2) for side in range(2)]

    def place_of(side, which, slot):
        return (4 * side + 2 * which + slot) * length

    def forward(side, slot, start, size):
        block = 0 if slot == 0 else 1 + side
        result = None
        for which in range(2):
            gate_in = dot_nt(
                tokens[block, pl.ds(start, size)], fc_sets[side, which]
            ) + bias[side][which]
            value, rate = gelu_both(gate_in)
            value = value.astype(bf16)
            rows = pl.ds(place_of(side, which, slot) + start, size)
            active[rows] = value
            slope[rows] = rate
            value = dot_nn(value, proj_sets[side, which])
            result = value if result is None else result + value
        return result

    scatter = PairScatter(part_ffn, inbox_ffn, send, recv, sems(4), near)
    own_part = forward(0, 0, 0, length)
    for copy in weights_sib + weights_on:
        copy.wait_recv()
    own_part = own_part + forward(1, 0, 0, length)
    for side, part in pieces:
        gather.wait(side, part)
        scatter.put(side, part, forward(side, 1, part * half, half))

    count = 2 * length
    mean_at = sems(len(sharers))
    to_sharers = [
        push(means.at[0], means.at[number], send.at[mean_at + k], recv.at[mean_at + number], target)
        for k, (number, target) in enumerate(sharers)
    ]
    mean_waits = [
        push(means.at[0], means.at[number], send.at[mean_at], recv.at[mean_at + number], to_sib)
        for number in range(4)
    ]

    @pl.when(root)
    def _():
        means[0] = jnp.zeros(means.shape[1:], f32)
        token_sum = total(tokens[0].astype(f32)) + total(tokens[1].astype(f32))
        unit_sum = total(active[pl.ds(place_of(0, 0, 0), count)].astype(f32))
        means[0, 0:1] = (token_sum * (1.0 / count)).astype(bf16).astype(f32)
        means[0, 1:2, :units] = (unit_sum * (1.0 / count)).astype(bf16).astype(f32)
        for copy in to_sharers:
            copy.start()

    for copy in teacher_in:
        copy.wait_recv()
    target = softmax_half(teacher_all[...].reshape(length, width).astype(f32))
    group = groups_ref[z]
    seq_weight = jnp.where(z < counts_ref[0], weight_ref[group], 0.0)
    out_low = teacher_all
    gather_two = PairGather(grad_y_all, send, recv, sems(4), near)
    half_blocks = blocks // 2
    for part in range(2):
        rows = slice(part * half, (part + 1) * half)
        block_out = hidden_buf[rows] + own_part[rows] + vec_ref[11:12] + scatter.collect(part)
        own_grad_y = (seq_weight * (width / TEMPER)) * (softmax_half(block_out) - target[rows])
        grad_y[rows] = own_grad_y
        grad_y_all[0, pl.ds(part * half, half)] = own_grad_y.astype(bf16)
        gather_two.start(part)
        out_low[pl.ds(part * half_blocks, half_blocks)] = block_out.astype(bf16).reshape(
            half_blocks, positions, width
        )
    back_out, back_in = token_exchange(out_low, out_back_ref)
    for copy in back_out:
        copy.start()
    out_back_ref[z] = out_low[z]

    def backward(side, slot, start, size):
        block = 0 if slot == 0 else 1 + side
        result = None
        for which in range(2):
            rows = pl.ds(place_of(side, which, slot) + start, size)
            grad_active = dot_nt(grad_y_all[block, pl.ds(start, size)], proj_sets[side, which])
            value = (grad_active * slope[rows]).astype(bf16)
            grad_gate[rows] = value
            value = dot_nn(value, fc_sets[side, which])
            result = value if result is None else result + value
        return result

    scatter.finish()
    scatter_two = PairScatter(part_ffn, inbox_ffn, send, recv, sems(4), near)
    own_part = backward(0, 0, 0, length) + backward(1, 0, 0, length)
    for side, part in pieces:
        gather_two.wait(side, part)
        scatter_two.put(side, part, backward(side, 1, part * half, half))

    @pl.when(jnp.logical_not(root))
    def _():
        mean_waits[0].wait_recv()

    for copy in mean_waits[1:]:
        copy.wait_recv()

    plane_at, chunk_at = sems(16), sems(16)

    def plane_source(goal, chunk=0):
        if goal == 2:
            return att_sum.at[pl.ds(n_qkv, n_out)]
        return att_sum.at[pl.ds(chunk * n_out, n_out)]

    def plane_copy(source, goal, chunk=0):
        if goal == 1:
            index = chunk_at + 4 * source + chunk
            rows = pl.ds(chunk * n_out, n_out)
            if source == 3 and chunk < 2:
                return push(
                    plane_source(goal, chunk), chain_in.at[1, rows], send.at[index],
                    recv.at[index], {"blk": 2},
                )
        else:
            index = plane_at + 4 * source + goal
            rows = pl.ds(0, sizes[goal])
        return push(
            plane_source(goal, chunk), plane_in.at[(source - goal) % 4 - 1, rows], send.at[index],
            recv.at[index], {"blk": goal},
        )

    chunk_count = n_qkv // n_out

    def send_plane(goal, chunk=0):
        for source in range(4):
            if source != goal and ((goal, source) != (1, 2) or chunk == 2):
                @pl.when(z == source)
                def _():
                    plane_copy(source, goal, chunk).start()

    def add_chunk(chunk):
        @pl.when(z == 2)
        def _():
            plane_copy(3, 1, chunk).wait_recv()
            rows = pl.ds(chunk * n_out, n_out)
            att_sum[rows] = (
                att_sum[rows].astype(f32) + chain_in[1, rows].astype(f32)
            ).astype(bf16)
            plane_copy(2, 1, chunk).start()

    at = sems(4)
    ffn_swap, ffn_near = [], []
    for i, (grads, held) in enumerate(((fc_grads, fc_sets), (proj_grads, proj_sets))):
        ffn_swap.append(
            push(grads.at[1], swap_ffn.at[i], send.at[at + i], recv.at[at + i], to_sib)
        )
        ffn_near.append(
            push(
                held.at[1, 0], ffn_from.at[i], send.at[at + 2 + i], recv.at[at + 2 + i],
                {"dp": weight_near},
            )
        )

    def pass_ffn(i):
        ffn_swap[i].wait_recv()
        grads, held = ((fc_grads, fc_sets), (proj_grads, proj_sets))[i]
        held[1, 0] = (grads[0, 1].astype(f32) + swap_ffn[i, 1].astype(f32)).astype(bf16)
        ffn_near[i].start()

    chain_at = sems(4)
    far_plane, add_plane, near_plane, goal_plane = (0, 3), (1, 2), (2, 1), (3, 0)

    def chain_copy(i, source):
        slot = 1 if source == add_plane[i] else 0
        goal = add_plane[i] if source == far_plane[i] else goal_plane[i]
        number = chain_at + 2 * i + slot
        return push(
            ffn_sum.at[i], chain_in.at[slot], send.at[number], recv.at[number], {"blk": goal}
        )

    def first_hop(i):
        @pl.when(jnp.logical_or(z == far_plane[i], z == near_plane[i]))
        def _():
            @pl.when(z == far_plane[i])
            def _():
                chain_copy(i, far_plane[i]).start()

            @pl.when(z == near_plane[i])
            def _():
                chain_copy(i, near_plane[i]).start()

    def second_hop(i):
        @pl.when(z == add_plane[i])
        def _():
            chain_copy(i, far_plane[i]).wait_recv()
            ffn_sum[i] = (ffn_sum[i].astype(f32) + chain_in[0].astype(f32)).astype(bf16)
            chain_copy(i, add_plane[i]).start()

    def sum_ffn(i):
        ffn_near[i].wait_recv()
        grads = (fc_grads, proj_grads)[i]
        ffn_sum[i] = (
            grads[0, 0].astype(f32) + swap_ffn[i, 0].astype(f32) + ffn_from[i].astype(f32)
        ).astype(bf16)
        first_hop(i)

    def shard_rows(ref, side, which):
        return ref[pl.ds(place_of(side, which, 0), count)]

    def both_blocks(ref, side):
        return jnp.concatenate([ref[0], ref[1 + side]], axis=0)

    gate_sums = {}

    def proj_side(side):
        grads = both_blocks(grad_y_all, side)
        for which in range(2):
            center = means[2 * which + side, 1:2, :units]
            values = (shard_rows(active, side, which).astype(f32) - center).astype(bf16)
            proj_grads[side, which] = dot_tn(values, grads).astype(bf16)

    def fc_side(side):
        block = both_blocks(tokens, side).astype(f32)
        for which in range(2):
            gate = shard_rows(grad_gate, side, which)
            gate_sums[side, which] = total(gate.astype(f32))
            center = means[2 * which + side, 0:1]
            fc_grads[side, which] = dot_tn(gate, (block - center).astype(bf16)).astype(bf16)

    proj_side(1)
    ffn_swap[1].start()
    proj_side(0)
    fc_side(1)
    ffn_swap[0].start()
    pass_ffn(1)
    fc_side(0)

    grad_normed = own_part + jnp.concatenate(
        [scatter_two.collect(0), scatter_two.collect(1)], axis=0
    )
    own_grad_y = grad_y[...]
    unit_two, scale_two = norm_parts(hidden_buf[...])
    back, gain_row, shift_row = norm_back(unit_two, scale_two, vec_ref[5:6], grad_normed)
    grad_hidden = own_grad_y + back
    low_hidden = grad_hidden.astype(bf16)
    hidden_sum = total(low_hidden.astype(f32))
    pass_ffn(0)
    rows_own[...] = jnp.zeros_like(rows_own)
    rows_own[4:5] = total(grad_hidden)
    rows_own[5:6] = gain_row[None]
    rows_own[6:7] = shift_row[None]
    blank = jnp.zeros((1, units), f32)

    def in_order(first, second):
        return jnp.where(
            core == 0,
            jnp.concatenate([first, second], axis=1),
            jnp.concatenate([second, first], axis=1),
        )

    rows_own[pl.ds(7 + chip, 1), :] = in_order(gate_sums[0, 0], gate_sums[1, 0])
    rows_own[pl.ds(7 + near_chips[1], 1), :] = in_order(gate_sums[0, 1], blank)
    rows_own[pl.ds(7 + near_chips[0], 1), :] = in_order(blank, gate_sums[1, 1])
    rows_own[11:12] = total(own_grad_y)
    rows_own[14:15] = total(own_grad_y.astype(bf16).astype(f32))
    grad_y[...] = grad_hidden

    out_grads[...] = dot_tn(low_hidden, att_low[...]).astype(bf16)
    at_swap = sems(16)

    def swap_copy(chunk, slot):
        owner = peers[slot] + 1 - 2 * core
        if chunk == 0:
            source = out_grads.at[pl.ds(pl.multiple_of(owner * n_out, 16), n_out)]
        else:
            start = owner * n_qkv + (chunk - 1) * n_out
            source = qkv_grads.at[pl.ds(pl.multiple_of(start, 16), n_out)]
        index = at_swap + 4 * chunk + slot
        return push(source, swap_att.at[chunk, slot], send.at[index], recv.at[index], to_sib)

    def own_rows(chunk, slot):
        if chunk == 0:
            return out_grads[pl.ds(pl.multiple_of(peers[slot] * n_out, 16), n_out)]
        start = peers[slot] * n_qkv + (chunk - 1) * n_out
        return qkv_grads[pl.ds(pl.multiple_of(start, 16), n_out)]

    swaps = [[swap_copy(chunk, slot) for slot in range(4)] for chunk in range(chunk_count + 1)]
    scatters = [
        PlaneScatter(proj_grads.at[c // 2, c % 2], inbox_att.at[c], send, recv, sems(6), xn, yn)
        for c in range(chunk_count + 1)
    ]

    def start_swap(chunk):
        for slot in (3, 2, 1, 0):
            swaps[chunk][slot].start()

    def put_chunk(chunk):
        for slot in (3, 2, 1, 0):
            swaps[chunk][slot].wait_recv()
            scatters[chunk].put(
                slot,
                own_rows(chunk, slot).astype(f32) + swap_att[chunk, slot].astype(f32),
            )

    def collect_chunk(chunk):
        rows = pl.ds(n_qkv if chunk == 0 else (chunk - 1) * n_out, n_out)
        att_sum[rows] = scatters[chunk].collect().astype(bf16)
        send_plane(2 if chunk == 0 else 1, max(chunk - 1, 0))

    start_swap(0)
    sum_ffn(1)
    ffn_swap[1].wait_send()
    grad_att = dot_nn(low_hidden, full_out[...]).astype(bf16)
    att_grad[...] = grad_att
    put_chunk(0)

    def pair_backward(pair):
        lanes = pl.ds(pl.multiple_of(pair * pair_width, pair_width), pair_width)
        queries, keys, values = qkv[0, :, lanes], qkv[1, :, lanes], qkv[2, :, lanes]
        grads = att_grad[:, lanes]
        product = grads.astype(f32) * attended[:, lanes]
        found = []
        for side in range(2):
            weights = probs[2 * pair + side]
            delta = jnp.sum(only(product, side), axis=-1, keepdims=True)
            grad_probs = dot_nt(only(grads, side), values)
            grad_scores = (weights * (grad_probs - delta)).astype(bf16)
            found.append(
                (
                    dot_nn(grad_scores, keys) * 0.125,
                    dot_tn(grad_scores, queries) * 0.125,
                    dot_tn(weights.astype(bf16), grads),
                )
            )
        for part in range(3):
            start = pl.multiple_of(part * width + pair * pair_width, pair_width)
            grad_mixed[:, pl.ds(start, pair_width)] = jnp.where(
                sides[0], found[0][part], found[1][part]
            ).astype(bf16)

    pl.loop(0, 2, unroll=2)(pair_backward)
    sum_ffn(0)
    pl.loop(2, pair_count, unroll=4)(pair_backward)
    scatters[0].relay()
    second_hop(1)
    mixed_sum = total(grad_mixed[...].astype(f32))
    strip = width // 2

    @pl.loop(0, full_qkv.shape[0] // strip, unroll=2)
    def _(step):
        rows = pl.ds(pl.multiple_of(step * strip, strip), strip)
        qkv_grads[rows] = dot_tn(grad_mixed[:, rows], normed[...]).astype(bf16)

    for chunk in range(1, chunk_count + 1):
        start_swap(chunk)
    collect_chunk(0)
    for chunk in range(1, chunk_count + 1):
        put_chunk(chunk)

    grad_one = dot_nn(grad_mixed[...], full_qkv[...])
    scatters[1].relay()
    second_hop(0)
    unit_one, scale_one = norm_parts(x_all[...].reshape(length, width).astype(f32))
    back, gain_row, shift_row = norm_back(unit_one, scale_one, vec_ref[0:1], grad_one)
    grad_ref[...] = (grad_y[...] + back).astype(bf16).reshape(grad_ref.shape)
    scatters[2].relay()
    collect_chunk(1)
    rows_own[0:1] = gain_row[None]
    rows_own[1:2] = shift_row[None]
    rows_own[2:3] = mixed_sum[:, :width]
    rows_own[3:4] = mixed_sum[:, 2 * width :]
    for rank in range(8):
        rows_own[16 + rank : 17 + rank, :n_qkv] = mixed_sum[:, rank * n_qkv : (rank + 1) * n_qkv]
        rows_own[16 + rank : 17 + rank, units : units + n_out] = hidden_sum[
            :, rank * n_out : (rank + 1) * n_out
        ]

    at = sems(8)
    row_sends, row_waits = [], []
    for k in range(1, ranks):
        row_sends.append(
            push(rows_own, rows_in.at[dp], send.at[at + k], recv.at[at + dp], {"dp": turn(k)})
        )
        source = turn(k)
        row_waits.append(
            push(rows_own, rows_in.at[source], send.at[at + k], recv.at[at + source], to_sib)
        )
        row_sends[-1].start()
    rows_in[dp] = rows_own[...]
    scatters[3].relay()
    collect_chunk(2)
    add_chunk(0)
    for copy in row_waits:
        copy.wait_recv()
    rows_sum = rows_in[0]
    for k in range(1, ranks):
        rows_sum = rows_sum + rows_in[k]
    rows_plane[z] = rows_sum
    plane_rows, plane_rows_in = token_exchange_rows(rows_plane, z, plane, planes, sems, send, recv)
    for copy in plane_rows:
        copy.start()
    add_chunk(1)
    collect_chunk(3)
    for copy in plane_rows_in:
        copy.wait_recv()
    every_row = rows_plane[0]
    for k in range(1, planes):
        every_row = every_row + rows_plane[k]
    total_ref[...] = every_row
    centers_ref[...] = means[0]
    centers_ref[2:3] = center_one
    centers_ref[3:4] = center_out

    for goal in range(4):
        @pl.when(z == goal)
        def _():
            size = sizes[goal]
            if goal in (0, 3):
                i = 1 - goal // 3
                for source in (near_plane[i], add_plane[i]):
                    chain_copy(i, source).wait_recv()
                value = ffn_sum[i].astype(f32) + (
                    chain_in[0].astype(f32) + chain_in[1].astype(f32)
                )
            else:
                value = (att_sum[:n_qkv] if goal == 1 else att_sum[n_qkv:]).astype(f32)
                for source in range(4):
                    if source == goal:
                        continue
                    through = (goal, source) == (1, 3)
                    for chunk in range(2 if through else 0, chunk_count if goal == 1 else 1):
                        plane_copy(source, goal, chunk).wait_recv()
                    slot = (source - goal) % 4 - 1
                    if through:
                        part = plane_in[slot, 2 * n_out : size].astype(f32)
                        blank = jnp.zeros((2 * n_out, width), f32)
                        value = value + jnp.concatenate([blank, part], axis=0)
                    else:
                        value = value + plane_in[slot, :size].astype(f32)
            if size < units:
                sums_ref[size:] = jnp.zeros((units - size, width), bf16)
            sums_ref[:size] = value.astype(bf16)
            for other in (1, 2):
                if other != goal:
                    for chunk in range(chunk_count if other == 1 else 1):
                        plane_copy(goal, other, chunk).wait_send()
            for i in range(2):
                if goal != goal_plane[i]:
                    chain_copy(i, goal).wait_send()

    for copy in back_in:
        copy.wait_recv()
    for copy in (
        inputs_out + teacher_out + weights_sib + weights_near + weights_on + back_out + ffn_swap[:1]
        + ffn_near + row_sends + plane_rows
        + [copy for chunk in swaps for copy in chunk]
    ):
        copy.wait_send()
    for item in (gather_qkv, gather_out, gather, gather_two, scatter_two, *scatters):
        item.finish()

    @pl.when(root)
    def _():
        for copy in to_sharers:
            copy.wait_send()


def token_exchange_rows(ref, z, plane, planes, sems, send, recv):
    at = sems(8)
    sends, waits = [], []
    for k in range(1, planes):
        other = plane(k)
        sends.append(
            push(ref.at[z], ref.at[z], send.at[at + k], recv.at[at + z], {"blk": other})
        )
        waits.append(
            push(ref.at[other], ref.at[other], send.at[at + k], recv.at[at + other], {"blk": other})
        )
    return sends, waits


def token_pass(counts, groups, group_weight, inputs, teacher, w_qkv, w_out, w_fc, w_proj, vectors):
    blocks, positions, width = inputs.shape
    length = blocks * positions
    n_qkv, n_out, units = w_qkv.shape[0], w_out.shape[0], w_proj.shape[0]
    chunks = 1 + n_qkv // n_out
    tokens = pltpu.VMEM((3, length, width), bf16)
    pair = pltpu.VMEM((2, length, width), bf16)
    low_rows = pltpu.VMEM((units, width), bf16)
    two_rows = pltpu.VMEM((2, units, width), bf16)
    four_rows = pltpu.VMEM((2, 2, units, width), bf16)
    unit_rows = 8 * length
    row_count = 24
    back = jax.ShapeDtypeStruct((blocks, positions, width), bf16)
    return pl.pallas_call(
        functools.partial(token_kernel, (units, n_qkv, n_out, units)),
        out_shape=(
            back, back,
            jax.ShapeDtypeStruct((units, width), bf16),
            jax.ShapeDtypeStruct((row_count, width), f32),
            jax.ShapeDtypeStruct((8, width), f32),
        ),
        in_specs=[SMEM_SPEC] * 3 + [VMEM_SPEC] * 4 + [ANY_SPEC] * 2 + [VMEM_SPEC],
        out_specs=(VMEM_SPEC,) * 5,
        scratch_shapes=[
            pltpu.VMEM((blocks, positions, width), bf16),
            pltpu.VMEM((blocks, positions, width), bf16),
            pltpu.VMEM((8 * n_qkv, width), bf16),
            pltpu.VMEM((8 * n_out, width), bf16),
            pltpu.VMEM((length, width), bf16),
            pltpu.VMEM((3, length, width), bf16),
            pltpu.VMEM((H, length, length), f32),
            pltpu.VMEM((length, width), f32),
            pltpu.VMEM((length, width), bf16),
            four_rows, four_rows,
            pltpu.VMEM((2 * length, width), f32),
            tokens,
            pltpu.VMEM((unit_rows, units), bf16),
            pltpu.VMEM((unit_rows, units), f32),
            tokens,
            pltpu.VMEM((unit_rows, units), bf16),
            pair, pair,
            pltpu.VMEM((4, 8, width), f32),
            four_rows, four_rows, four_rows, two_rows, two_rows, two_rows,
            pltpu.VMEM((length, width), bf16),
            pltpu.VMEM((length, 3 * width), bf16),
            pltpu.VMEM((8 * n_qkv, width), bf16),
            pltpu.VMEM((8 * n_out, width), bf16),
            pltpu.VMEM((chunks, 4, n_out, width), bf16),
            pltpu.VMEM((chunks, 6, n_out // 2, width), bf16),
            low_rows,
            pltpu.VMEM((3, n_qkv, width), bf16),
            pltpu.VMEM((row_count, width), f32),
            pltpu.VMEM((8, row_count, width), f32),
            pltpu.VMEM((4, row_count, width), f32),
            pltpu.SemaphoreType.DMA((2,)),
            pltpu.SemaphoreType.DMA((220,)),
            pltpu.SemaphoreType.DMA((220,)),
        ],
        compiler_params=pltpu.CompilerParams(
            collective_id=0, has_side_effects=True, vmem_limit_bytes=VMEM_BYTES
        ),
        name="tokens",
    )(counts, groups, group_weight, inputs, teacher, w_qkv, w_out, w_fc, w_proj, vectors)


def split_pair(values):
    upper = values.astype(bf16)
    return upper, (values - upper.astype(f32)).astype(bf16)


class Chain:
    def __init__(self, ref, sizes, send, recv, sems):
        self.ref, self.sizes, self.send, self.recv = ref, sizes, send, recv
        self.begin = (sems(32), sems(32))
        self.arrivals = [[] for _ in sizes]
        planes = len(sizes)
        for way in range(2):
            ahead = 1 if way == 0 else -1
            plane = 0 if way == 0 else planes - 1
            passing = []
            while 0 <= plane + ahead < planes:
                queue = [(0.0, plane, index) for index in range(self.chunks(plane))] + passing
                clock, passing = 0.0, []
                for ready, source, index in sorted(queue):
                    clock = max(clock, ready) + sizes[source] / self.chunks(source)
                    passing.append((clock + 32.0, source, index))
                plane += ahead
                self.arrivals[plane] += [(*item, way) for item in passing]
        for item in self.arrivals:
            item.sort()

    def chunks(self, source):
        return 2 if self.sizes[source] <= 96 else 6

    def move(self, source, index, goal, way):
        rows_each = self.sizes[source] // self.chunks(source)
        area = self.ref.at[source, pl.ds(index * rows_each, rows_each)]
        number = self.begin[way] + 8 * source + index
        return push(area, area, self.send.at[number], self.recv.at[number], {"blk": goal})

    def onward(self, plane, way):
        goal = plane + (1 if way == 0 else -1)
        return goal if 0 <= goal < len(self.sizes) else None

    def start(self, plane, index):
        if index < self.chunks(plane):
            for way in range(2):
                goal = self.onward(plane, way)
                if goal is not None:
                    self.move(plane, index, goal, way).start()

    def hop(self, plane, first, last):
        count = len(self.arrivals[plane])
        for _, source, index, way in self.arrivals[plane][count * first // 4 : count * last // 4]:
            self.move(source, index, plane, way).wait_recv()
            goal = self.onward(plane, way)
            if goal is not None:
                self.move(source, index, goal, way).start()

    def finish(self, plane):
        own = [(0.0, plane, index, way) for index in range(self.chunks(plane)) for way in range(2)]
        for _, source, index, way in own + self.arrivals[plane]:
            goal = self.onward(plane, way)
            if goal is not None:
                self.move(source, index, goal, way).wait_send()


def muon_kernel(
    sizes,
    own_ref, total_in_ref, centers_in_ref, grad_ref,
    mom_proj_ref, mom_qkv_ref, mom_out_ref, mom_fc_ref,
    sums_ref, update_ref, grad_back_ref,
    total_ref, centers_ref, small_sems,
    gram_own, gram_other, gram_swap, gram_in, gram_all,
    gram, gram_up, gram_low, poly_up, poly_low, half, half_up, half_low,
    iterate, iter_up, iter_low, mom_wide, mom_rows, mom_sems, send, recv,
):
    units, width = own_ref.shape
    dp, core, chip, sib, xn, yn = place()
    z = lax.axis_index("blk")
    planes = lax.axis_size("blk")
    small_in = [
        pltpu.make_async_copy(source, target, small_sems.at[i])
        for i, (source, target) in enumerate(
            (
                (own_ref, sums_ref.at[z]), (total_in_ref, total_ref),
                (centers_in_ref, centers_ref), (grad_ref.at[z], grad_back_ref.at[z]),
            )
        )
    ]
    for copy in small_in:
        copy.start()
    diag = xn + yn - dp
    peers = (dp, xn, yn, diag)
    to_sib = {"dp": sib}
    sems = Sems()

    def each_plane(action):
        for plane in range(4):
            @pl.when(z == plane)
            def _():
                action(plane)

    mom_in = (
        (mom_proj_ref, mom_rows),
        (mom_qkv_ref, mom_rows.at[pl.ds(0, sizes[1])]),
        (mom_out_ref, mom_rows.at[pl.ds(0, sizes[2])]),
        (mom_fc_ref, mom_wide),
    )

    def load_momentum(plane):
        pltpu.make_async_copy(*mom_in[plane], mom_sems.at[plane]).start()

    def take_momentum(plane):
        pltpu.make_async_copy(*mom_in[plane], mom_sems.at[plane]).wait()
        if plane == 3:
            mom_rows[...] = mom_wide[...].T
        if sizes[plane] < units:
            mom_rows[sizes[plane] :] = jnp.zeros((units - sizes[plane], width), f32)

    each_plane(load_momentum)
    greet(
        [to_sib, {"dp": xn}, {"dp": yn}, {"dp": diag}]
        + [{"blk": lax.rem(z + k, planes)} for k in range(1, planes)]
    )
    small_in[0].wait()
    sums_chain = Chain(sums_ref, sizes, send, recv, sems)
    each_plane(lambda plane: [sums_chain.start(plane, index) for index in range(6)])
    at = sems(8)
    back_out, back_in = [], []
    for k in range(1, planes):
        other = lax.rem(z + k, planes)
        back_out.append(
            push(
                grad_ref.at[other], grad_back_ref.at[z], send.at[at + k], recv.at[at + z],
                {"blk": other},
            )
        )
        back_in.append(
            push(
                grad_ref.at[other], grad_back_ref.at[other], send.at[at + k],
                recv.at[at + other], {"blk": other},
            )
        )
        back_out[-1].start()
    for copy in small_in[1:]:
        copy.wait()
    own_total = total_ref[pl.ds(16 + dp, 1), :]
    gate_row = total_ref[pl.ds(7 + chip, 1), :]

    def by_core(row):
        return jnp.where(core == 0, row[:, :units], row[:, units:])

    sum_row = jnp.where(
        z == 3, by_core(gate_row), jnp.where(z == 1, own_total[:, :units], own_total[:, units:])
    )
    mean_row = jnp.where(
        z == 3, centers_ref[0:1], jnp.where(z == 1, centers_ref[2:3], centers_ref[3:4])
    )
    left = jnp.where(
        z == 0,
        jnp.broadcast_to(centers_ref[1:2, :units], (8, units)),
        row_splits(sum_row).astype(f32),
    ).astype(bf16)
    right = jnp.where(
        z == 0,
        row_splits(total_ref[14:15]).astype(f32),
        jnp.broadcast_to(mean_row, (8, width)),
    ).astype(bf16)
    each_plane(take_momentum)
    value = MOMENT_DECAY * mom_rows[...] + (sums_ref[z].astype(f32) + dot_tn(left, right))
    iterate[...] = value
    value_up, value_low = split_pair(value)
    iter_up[...] = value_up
    iter_low[...] = value_low

    tile = gram_own.shape[1]
    quarter = tile // 4
    pairs = [(0, 0), (0, 1), (0, 2), (1, 1), (1, 2), (2, 2)]

    def gram_block(side, index):
        (i, j), (k, l) = pairs[index], pairs[3 + index]
        first = pl.ds(pl.multiple_of(jnp.where(side == 0, i, k) * tile, tile), tile)
        second = pl.ds(pl.multiple_of(jnp.where(side == 0, j, l) * tile, tile), tile)
        upper, lower = iter_up[:, first], iter_low[:, first]
        return dot_tn(
            jnp.concatenate([upper, upper, lower], axis=0),
            jnp.concatenate([iter_up[:, second], iter_low[:, second], iter_up[:, second]], axis=0),
        )

    at = sems(3)
    gram_sib = [
        push(gram_other.at[k], gram_swap.at[k], send.at[at + k], recv.at[at + k], to_sib)
        for k in range(3)
    ]
    for k in range(3):
        gram_other[k] = gram_block(1 - core, k)
        gram_sib[k].start()
    others = (chip, lax.div(xn, 2), lax.div(yn, 2), lax.div(diag, 2))
    at = sems(12)

    def quarter_of(item):
        return pl.ds(pl.multiple_of(item * quarter, quarter), quarter)

    gram_sends = []
    for k in range(3):
        gram_own[k] = gram_block(core, k)
    for k in range(3):
        gram_sib[k].wait_recv()
        gram_own[k] = gram_own[k] + gram_swap[k]
        for slot in (3, 2, 1):
            index = at + 4 * k + slot
            copy = push(
                gram_own.at[k, quarter_of(others[slot])], gram_in.at[slot, k], send.at[index],
                recv.at[index], {"dp": peers[slot]},
            )
            copy.start()
            gram_sends.append(copy)
    at = sems(12)
    at_sib = sems(4)
    gram_out = []
    for k in range(3):
        for copy in gram_sends[3 * k : 3 * k + 3]:
            copy.wait_recv()
        gram_all[core, chip, k] = (
            gram_own[k, quarter_of(chip)] + gram_in[1, k] + (gram_in[2, k] + gram_in[3, k])
        )
        for slot in (3, 2, 1):
            area = gram_all.at[core, chip, k]
            index = at + 4 * k + slot
            copy = push(area, area, send.at[index], recv.at[index], {"dp": peers[slot]})
            copy.start()
            gram_out.append(copy)

    def gram_copy(side, slot):
        area = gram_all.at[side, others[slot]]
        index = at_sib + slot
        return push(area, area, send.at[index], recv.at[index], to_sib)

    gram_on = [gram_copy(core, slot) for slot in range(4)]
    gram_on[0].start()
    for slot in (1, 2, 3):
        for k in range(3):
            area = gram_all.at[core, others[slot], k]
            index = at + 4 * k + slot
            push(area, area, send.at[index], recv.at[index], {"dp": peers[slot]}).wait_recv()
        gram_on[slot].start()
    for slot in range(4):
        gram_copy(1 - core, slot).wait_recv()

    every = [
        jnp.concatenate([gram_all[index // 3, item, index % 3] for item in range(4)], axis=0)
        for index in range(6)
    ]
    row_id = lax.broadcasted_iota(jnp.int32, (tile, tile), 0)
    col_id = lax.broadcasted_iota(jnp.int32, (tile, tile), 1)
    diagonal = jnp.where(row_id == col_id, every[0] + every[3] + every[5], 0.0)
    trace = jnp.sum(jnp.sum(diagonal, axis=1, keepdims=True), axis=0, keepdims=True)
    scale = 1.0 / (jnp.sqrt(trace) + 1e-07)

    value = iterate[...] * scale
    iterate[...] = value
    iter_up[...] = value.astype(bf16)
    def block(i, j):
        return slice(i * tile, (i + 1) * tile), slice(j * tile, (j + 1) * tile)

    def mirror(ref, column, values):
        ref[: (column + 1) * tile, block(0, column)[1]] = values
        for i in range(column):
            ref[block(column, i)] = values[i * tile : (i + 1) * tile].T

    def mirror_pair(pair, column, values):
        for ref, part in zip(pair, split_pair(values)):
            mirror(ref, column, part)

    def left_rows(pair, column):
        upper, lower = (ref[: (column + 1) * tile] for ref in pair)
        return jnp.concatenate([upper, upper, lower], axis=1)

    def right_columns(pair, column):
        upper, lower = (ref[:, block(0, column)[1]] for ref in pair)
        return jnp.concatenate([upper, lower, upper], axis=0)

    gram_pair, poly_pair, half_pair = (gram_up, gram_low), (poly_up, poly_low), (half_up, half_low)
    for index, (i, j) in enumerate(pairs):
        gram[block(i, j)] = every[index] * (scale * scale)
    for column in range(3):
        mirror_pair(gram_pair, column, gram[: (column + 1) * tile, block(0, column)[1]])
    each_plane(lambda plane: sums_chain.hop(plane, 0, 2))
    update_chain = Chain(update_ref, sizes, send, recv, sems)

    for sweep in range(ITERS):
        first, last = sweep == 0, sweep == ITERS - 1
        for column in range(3):
            rows, lanes = slice(0, (column + 1) * tile), block(0, column)[1]
            if first:
                square = dot_nn(left_rows(gram_pair, column), right_columns(gram_pair, column))
            else:
                square = dot_nn(gram_up[rows], gram_up[:, lanes])
            values = POLY_SECOND * gram[rows, lanes] + POLY_THIRD * square
            if first:
                mirror_pair(poly_pair, column, values)
            else:
                mirror(poly_up, column, values.astype(bf16))

        if last:
            part = units // 3
            for index in range(3):
                rows = slice(index * part, (index + 1) * part)
                values = POLY_FIRST * iterate[rows] + dot_nn(iter_up[rows], poly_up[...])
                update_ref[z, rows] = values.astype(bf16)
                each_plane(
                    lambda plane: [update_chain.start(plane, 2 * index + i) for i in range(2)]
                )
            continue

        for column in range(3):
            rows, lanes = slice(0, (column + 1) * tile), block(0, column)[1]
            if first:
                update = dot_nn(left_rows(poly_pair, column), right_columns(gram_pair, column))
            else:
                update = dot_nn(poly_up[rows], gram_up[:, lanes])
            values = POLY_FIRST * gram[rows, lanes] + update
            half[rows, lanes] = values
            if first:
                mirror_pair(half_pair, column, values)
            else:
                mirror(half_up, column, values.astype(bf16))

        for column in range(3):
            rows, lanes = slice(0, (column + 1) * tile), block(0, column)[1]
            if first:
                update = dot_nn(left_rows(half_pair, column), right_columns(poly_pair, column))
            else:
                update = dot_nn(half_up[rows], poly_up[:, lanes])
            values = POLY_FIRST * half[rows, lanes] + update
            gram[rows, lanes] = values
            mirror(gram_up, column, values.astype(bf16))

        values = POLY_FIRST * iterate[...] + dot_nn(iter_up[...], poly_up[...])
        iterate[...] = values
        iter_up[...] = values.astype(bf16)
        if sweep == 1:
            each_plane(lambda plane: sums_chain.hop(plane, 2, 3))
        elif sweep == 3:
            each_plane(lambda plane: sums_chain.hop(plane, 3, 4))

    def last_exchange(plane):
        update_chain.hop(plane, 0, 4)
        sums_chain.finish(plane)
        update_chain.finish(plane)

    each_plane(last_exchange)
    for copy in back_in:
        copy.wait_recv()
    for copy in back_out + gram_sends + gram_out + gram_on + gram_sib:
        copy.wait_send()


def muon(own, totals, centers, grad, moms, sizes):
    units, width = own.shape
    tile = width // 3
    low_rows = pltpu.VMEM((units, width), bf16)
    rows_f32 = pltpu.VMEM((units, width), f32)
    square_f32 = pltpu.VMEM((width, width), f32)
    square_low = pltpu.VMEM((width, width), bf16)
    blocks = pltpu.VMEM((3, tile, tile), f32)
    every = jax.ShapeDtypeStruct((4, units, width), bf16)
    return pl.pallas_call(
        functools.partial(muon_kernel, sizes),
        out_shape=(every, every, jax.ShapeDtypeStruct(grad.shape, bf16)),
        in_specs=[HBM_SPEC] * 4 + [ANY_SPEC] * 4,
        out_specs=(VMEM_SPEC,) * 3,
        scratch_shapes=[
            pltpu.VMEM(totals.shape, f32),
            pltpu.VMEM(centers.shape, f32),
            pltpu.SemaphoreType.DMA((4,)),
            blocks, blocks, blocks,
            pltpu.VMEM((4, 3, tile // 4, tile), f32),
            pltpu.VMEM((2, 4, 3, tile // 4, tile), f32),
            square_f32, square_low, square_low, square_low, square_low,
            square_f32, square_low, square_low,
            rows_f32, low_rows, low_rows,
            pltpu.VMEM(moms[3].shape, f32), rows_f32,
            pltpu.SemaphoreType.DMA((4,)),
            pltpu.SemaphoreType.DMA((168,)),
            pltpu.SemaphoreType.DMA((168,)),
        ],
        compiler_params=pltpu.CompilerParams(
            collective_id=1, has_side_effects=True, vmem_limit_bytes=VMEM_MUON
        ),
        name="muon",
    )(
        *[pltpu.with_memory_space_constraint(a, pltpu.HBM) for a in (own, totals, centers, grad)],
        *moms,
    )


def finish_kernel(
    sums_ref, updates_ref, total_ref, centers_ref, vec_ref, grad_ref, *rest
):
    tokens_ref, rest = rest[0], rest[1:]
    mom_refs, w_refs, mom_outs, w_outs, copy_outs = (rest[4 * i : 4 * i + 4] for i in range(5))
    grad_out_ref, vec_total_ref, vec_new_ref, tokens_out_ref = rest[20:24]
    mom_bufs, w_bufs, low_bufs = (rest[24 + 4 * i : 28 + 4 * i] for i in range(3))
    sems = rest[36]
    units = updates_ref.shape[1]
    dp, core, chip, _, _, _ = place()

    def by_core(row):
        return jnp.where(core == 0, row[:, :units], row[:, units:])

    own_total = total_ref[pl.ds(16 + dp, 1), :]
    sizes = (units, w_refs[1].shape[0], w_refs[2].shape[0], units)
    sums = (
        None,
        own_total[:, : sizes[1]],
        own_total[:, units : units + sizes[2]],
        by_core(total_ref[pl.ds(7 + chip, 1), :]),
    )
    rates = (
        RATE_PROJ * math.sqrt(FF / D), RATE_QKV * math.sqrt(QKV / D), RATE_OUT,
        RATE_FC * math.sqrt(FF / D),
    )
    centers = (None, centers_ref[2:3], centers_ref[3:4], centers_ref[0:1])
    stores = [pltpu.make_async_copy(tokens_ref, tokens_out_ref, sems.at[20])]
    stores[0].start()

    def leave(source, target, index):
        copy = pltpu.make_async_copy(source, target, sems.at[index])
        copy.start()
        stores.append(copy)

    for i in range(4):
        if i == 0:
            spike = dot_tn(row_repeat(centers_ref[1:2, :units]), row_splits(total_ref[14:15]))
            total = sums_ref[i].astype(f32) + spike
        elif i < 3:
            spike = dot_tn(row_splits(sums[i]), row_repeat(centers[i]))
            total = sums_ref[i, : sizes[i]].astype(f32) + spike
        else:
            spike = dot_tn(row_repeat(centers[i]), row_splits(sums[i]))
            total = sums_ref[i].astype(f32).T + spike
        mom_bufs[i][...] = MOMENT_DECAY * mom_refs[i][...] + total
        leave(mom_bufs[i], mom_outs[i], 8 + i)
        update = updates_ref[i, : sizes[i]].astype(f32)
        if i == 3:
            update = update.T
        new = w_refs[i][...] - rates[i] * update
        w_bufs[i][...] = new
        leave(w_bufs[i], w_outs[i], 12 + i)
        low_bufs[i][...] = new.astype(bf16)
        leave(low_bufs[i], copy_outs[i], 16 + i)

    grad_out_ref[...] = grad_ref[...].astype(f32)
    vec_total = total_ref[: vec_ref.shape[0]]
    vec_total_ref[...] = vec_total
    vec_new_ref[...] = vec_ref[...] - RATE_VEC * vec_total * lax.rsqrt(
        jnp.mean(vec_total * vec_total, axis=-1, keepdims=True) + NORM_EPS
    )
    for copy in stores:
        copy.wait()


def finish(sums, updates, totals, centers, vectors, grad, tokens, moms, weights):
    full = [jax.ShapeDtypeStruct(w.shape, f32) for w in weights]
    low = [jax.ShapeDtypeStruct(w.shape, bf16) for w in weights]
    return pl.pallas_call(
        finish_kernel,
        out_shape=(
            *full, *full, *low,
            jax.ShapeDtypeStruct(grad.shape, f32),
            jax.ShapeDtypeStruct(vectors.shape, f32),
            jax.ShapeDtypeStruct(vectors.shape, f32),
            jax.ShapeDtypeStruct(tokens.shape, bf16),
        ),
        in_specs=[VMEM_SPEC] * 6 + [ANY_SPEC] + [VMEM_SPEC] * 8,
        out_specs=(ANY_SPEC,) * 12 + (VMEM_SPEC,) * 3 + (ANY_SPEC,),
        scratch_shapes=[
            *[pltpu.VMEM(w.shape, f32) for w in weights],
            *[pltpu.VMEM(w.shape, f32) for w in weights],
            *[pltpu.VMEM(w.shape, bf16) for w in weights],
            pltpu.SemaphoreType.DMA((21,)),
        ],
        compiler_params=pltpu.CompilerParams(vmem_limit_bytes=VMEM_FINISH),
        name="finish",
    )(sums, updates, totals, centers, vectors, grad, tokens, *moms, *weights)


def per_device_any(
    inputs, teacher, counts, groups, group_weight, w_qkv, w_out, w_fc, w_proj,
    vectors, mom_qkv, mom_out, mom_fc, mom_proj,
):
    width = inputs.shape[-1]
    z = lax.axis_index("blk")
    dp = lax.axis_index("dp")

    low_qkv = w_qkv.T.astype(bf16)
    low_out = w_out.T.astype(bf16)
    low_fc = w_fc.T.astype(bf16)
    low_proj = w_proj.astype(bf16)
    full_qkv = lax.all_gather(low_qkv, "dp", axis=0, tiled=True)
    full_out = lax.all_gather(low_out, "dp", axis=0, tiled=True)

    x = lax.all_to_all(inputs, "blk", 0, 1, tiled=True)[0].astype(f32)
    target_in = lax.all_to_all(teacher, "blk", 0, 1, tiled=True)[0].astype(f32)
    length = x.shape[0]
    chosen = (groups[z] == jnp.arange(GROUPS, dtype=jnp.int32)).astype(f32)
    seq_weight = jnp.sum(chosen * group_weight) * (z < counts[0]).astype(f32)

    unit_one, scale_one = norm_parts(x)
    normed = (unit_one * vectors[0] + vectors[1]).astype(bf16)
    mixed = dot_nt(normed, full_qkv)
    queries = (mixed[:, :width] + vectors[2]).astype(bf16)
    keys = mixed[:, width : 2 * width].astype(bf16)
    values = (mixed[:, 2 * width :] + vectors[3]).astype(bf16)

    def heads(a):
        return a.reshape(length, H, HD).transpose(1, 0, 2)

    def flat(a):
        return a.transpose(1, 0, 2).reshape(length, width)

    q_h, k_h, v_h = heads(queries), heads(keys), heads(values)
    pos = jnp.arange(length, dtype=jnp.int32)
    visible = pos[None, :] <= pos[:, None]
    scores = jnp.einsum("hqd,hkd->hqk", q_h, k_h, preferred_element_type=f32) * 0.125
    scores = jnp.where(visible, scores, MASKED)
    peak = jnp.max(scores, axis=-1, keepdims=True)
    weights = jnp.exp(scores - peak)
    probs = weights / jnp.sum(weights, axis=-1, keepdims=True)
    probs_low = probs.astype(bf16)
    att_h = jnp.einsum("hqk,hkd->hqd", probs_low, v_h, preferred_element_type=f32)
    attended_low = flat(att_h).astype(bf16)
    hidden = x + dot_nt(attended_low, full_out) + vectors[4]
    unit_two, scale_two = norm_parts(hidden)
    normed_two = (unit_two * vectors[5] + vectors[6]).astype(bf16)

    token_total = length * lax.axis_size("dp") * lax.axis_size("blk")
    means = lax.psum(
        jnp.stack(
            [jnp.sum(rows.astype(f32), axis=0) for rows in (normed, attended_low, normed_two)]
        ),
        ("dp", "blk"),
    ) / token_total
    all_two = lax.all_gather(normed_two, "dp", axis=0, tiled=True)
    hidden_units = low_fc.shape[0]
    fc_rows = FF // D
    fc_bias = lax.dynamic_slice(
        vectors[7 : 7 + fc_rows].reshape(FF), (dp * hidden_units,), (hidden_units,)
    )
    gate_in = dot_nt(all_two, low_fc) + fc_bias
    active, slope = gelu_both(gate_in)
    active_low = active.astype(bf16)
    active_mean = lax.psum(jnp.sum(active_low.astype(f32), axis=0), "blk") / token_total
    part_out = dot_nn(active_low, low_proj).astype(bf16)
    block_out = (
        hidden
        + lax.psum_scatter(part_out, "dp", scatter_dimension=0, tiled=True).astype(f32)
        + vectors[7 + fc_rows]
    )
    student = jax.nn.softmax(block_out / TEMPER, axis=-1)
    target = jax.nn.softmax(target_in / TEMPER, axis=-1)
    grad_y = (seq_weight * (width / TEMPER)) * (student - target)
    grad_y_low = grad_y.astype(bf16)
    all_grad_y = lax.all_gather(grad_y_low, "dp", axis=0, tiled=True)
    grad_gate = (dot_nt(all_grad_y, low_proj) * slope).astype(bf16)
    part_two = dot_nn(grad_gate, low_fc).astype(bf16)
    grad_normed_two = lax.psum_scatter(
        part_two, "dp", scatter_dimension=0, tiled=True
    ).astype(f32)
    grad_fc_bias = jnp.sum(grad_gate.astype(f32), axis=0)
    sum_grad_y = jnp.sum(all_grad_y.astype(f32), axis=0)
    grad_proj = dot_tn(active_low, all_grad_y) - active_mean[:, None] * sum_grad_y
    grad_fc = dot_tn(grad_gate, all_two) - grad_fc_bias[:, None] * means[2]

    back_two, grad_gain_two, grad_bias_two = norm_back(
        unit_two, scale_two, vectors[5], grad_normed_two
    )
    grad_hidden = grad_y + back_two
    grad_hidden_low = grad_hidden.astype(bf16)
    sum_grad_hidden = jnp.sum(grad_hidden_low.astype(f32), axis=0)
    grad_out = dot_tn(grad_hidden_low, attended_low) - sum_grad_hidden[:, None] * means[1]
    grad_att = dot_nn(grad_hidden_low, full_out).astype(bf16)
    ga_h = heads(grad_att)
    delta = jnp.sum(ga_h.astype(f32) * att_h, axis=-1, keepdims=True)
    grad_probs = jnp.einsum("hqd,hkd->hqk", ga_h, v_h, preferred_element_type=f32)
    grad_scores = (probs * (grad_probs - delta)).astype(bf16)
    grad_q = jnp.einsum("hqk,hkd->hqd", grad_scores, k_h, preferred_element_type=f32) * 0.125
    grad_k = jnp.einsum("hqk,hqd->hkd", grad_scores, q_h, preferred_element_type=f32) * 0.125
    grad_v = jnp.einsum("hqk,hqd->hkd", probs_low, ga_h, preferred_element_type=f32)
    grad_mixed = jnp.concatenate([flat(grad_q), flat(grad_k), flat(grad_v)], axis=-1).astype(bf16)
    bias_sums = jnp.sum(grad_mixed.astype(f32), axis=0)
    grad_qkv = dot_tn(grad_mixed, normed) - bias_sums[:, None] * means[0]
    back_one, grad_gain_one, grad_bias_one = norm_back(
        unit_one, scale_one, vectors[0], dot_nn(grad_mixed, full_qkv)
    )
    grad_input = grad_hidden + back_one

    sum_qkv = lax.psum_scatter(grad_qkv.astype(bf16), "dp", scatter_dimension=0, tiled=True)
    sum_out = lax.psum_scatter(grad_out.astype(bf16), "dp", scatter_dimension=0, tiled=True)
    shard_sums = lax.psum(
        jnp.concatenate([sum_qkv, sum_out, grad_fc.astype(bf16), grad_proj.astype(bf16)]), "blk"
    ).astype(f32)
    vec_grad = jnp.concatenate(
        [
            jnp.stack(
                [
                    grad_gain_one, grad_bias_one, bias_sums[:width], bias_sums[2 * width :],
                    jnp.sum(grad_hidden, axis=0), grad_gain_two, grad_bias_two,
                ]
            ),
            lax.dynamic_update_slice(
                jnp.zeros((FF,), f32), grad_fc_bias, (dp * hidden_units,)
            ).reshape(fc_rows, width),
            jnp.stack(
                [
                    jnp.sum(grad_y, axis=0), bias_sums[width : 2 * width], sum_grad_hidden,
                    jnp.sum(grad_y_low.astype(f32), axis=0),
                ]
            ),
        ],
        axis=0,
    )
    vec_all = lax.psum(vec_grad, ("dp", "blk"))
    vec_total = vec_all[: vectors.shape[0]]
    sums_qkv = jnp.concatenate([vec_all[2], vec_all[12], vec_all[3]])

    n_qkv, n_out, n_fc = w_qkv.shape[1], w_out.shape[1], w_fc.shape[1]
    cuts = (0, n_qkv, n_qkv + n_out, n_qkv + n_out + n_fc, n_qkv + n_out + 2 * n_fc)
    def own(sums, count):
        return lax.dynamic_slice(sums, (dp * count,), (count,))[:, None]

    spikes = (
        own(sums_qkv, n_qkv) * means[0],
        own(vec_all[13], n_out) * means[1],
        own(vec_all[7 : 7 + fc_rows].reshape(FF), n_fc) * means[2],
        active_mean[:, None] * vec_all[14],
    )
    new_moms = [
        MOMENT_DECAY * mom + (shard_sums[low:high] + spike)
        for mom, low, high, spike in zip(
            (mom_qkv.T, mom_out.T, mom_fc.T, mom_proj), cuts[:-1], cuts[1:], spikes
        )
    ]
    stacked = jnp.stack(
        [jnp.pad(mom, ((0, n_fc - mom.shape[0]), (0, 0))) for mom in new_moms]
    )
    rows = lax.dynamic_index_in_dim(stacked, z, 0, keepdims=False)
    gram = lax.psum(three_pass(dot_tn, rows, rows), "dp")
    rows = newton_schulz(rows, gram)
    updates = lax.all_gather(rows.astype(bf16), "blk", axis=0).astype(f32)
    qkv_new = w_qkv - RATE_QKV * math.sqrt(QKV / D) * updates[0, :n_qkv].T
    out_new = w_out - RATE_OUT * updates[1, :n_out].T
    fc_new = w_fc - RATE_FC * math.sqrt(FF / D) * updates[2].T
    proj_new = w_proj - RATE_PROJ * math.sqrt(FF / D) * updates[3]
    vectors_new = vectors - RATE_VEC * vec_total * lax.rsqrt(
        jnp.mean(vec_total * vec_total, axis=-1, keepdims=True) + NORM_EPS
    )
    outputs = lax.all_to_all(block_out.astype(bf16)[None], "blk", 1, 0, tiled=True)
    input_grad = lax.all_to_all(grad_input.astype(bf16)[None], "blk", 1, 0, tiled=True)
    return (
        outputs,
        input_grad.astype(f32),
        new_moms[0].T,
        new_moms[1].T,
        new_moms[2].T,
        new_moms[3],
        qkv_new,
        out_new,
        fc_new,
        proj_new,
        qkv_new.astype(bf16),
        out_new.astype(bf16),
        fc_new.astype(bf16),
        proj_new.astype(bf16),
        vec_total,
        vectors_new,
    )


def per_device(
    inputs, teacher, counts, groups, group_weight, w_qkv, w_out, w_fc, w_proj,
    vectors, mom_qkv, mom_out, mom_fc, mom_proj,
):
    sizes = (w_fc.shape[1], w_qkv.shape[1], w_out.shape[1], w_proj.shape[0])
    outputs, grad, own, totals, centers = token_pass(
        counts, groups, group_weight, inputs, teacher, w_qkv.T, w_out.T, w_fc, w_proj, vectors
    )
    moms = (mom_proj, mom_qkv.T, mom_out.T, mom_fc)
    sums, updates, grads = muon(own, totals, centers, grad, moms, sizes)
    done = finish(
        sums, updates, totals, centers, vectors, grads, outputs, moms, (w_proj, w_qkv.T, w_out.T, w_fc)
    )

    def ordered(start):
        return (done[start + 1].T, done[start + 2].T, done[start + 3], done[start])

    return (done[15], done[12], *ordered(0), *ordered(4), *ordered(8), done[13], done[14])


def solution(mesh):
    token = P("dp", "blk", None)
    column = P(None, "dp")
    row = P("dp", None)
    in_specs = (
        token, token, P("dp"), P("dp"), P(), column, column, column, row, P(),
        column, column, column, row,
    )
    out_specs = (
        token, token, column, column, column, row, column, column, column, row,
        column, column, column, row, P(), P(),
    )
    body = per_device if dict(mesh.shape) == {"dp": 8, "blk": 4} else per_device_any
    return jax.shard_map(
        body, mesh=mesh, in_specs=in_specs, out_specs=out_specs, check_vma=False
    )
```

```python
import functools
import math

import jax
import jax.numpy as jnp
from jax import lax
from jax.experimental import pallas as pl
from jax.experimental.pallas import tpu as pltpu
from jax.sharding import PartitionSpec as P

D = 768
H = 12
HD = 64
QKV = 2304
FF = 3072
GROUPS = 8
ITERS = 5

NORM_EPS = 1e-05
TEMPER = 2.0
MOMENT_DECAY = 0.5
POLY_FIRST = 3.4445
POLY_SECOND = -4.775
POLY_THIRD = 2.0315
RATE_QKV = 1.0
RATE_OUT = 3.0
RATE_FC = 0.5
RATE_PROJ = 0.5
RATE_VEC = 0.3
MASKED = -1e30
GELU_SCALE = math.sqrt(2.0 / math.pi)
f32 = jnp.float32
bf16 = jnp.bfloat16
HIGHEST = lax.Precision.HIGHEST


def dot_nn(a, b):
    return lax.dot_general(a, b, (((1,), (0,)), ((), ())), preferred_element_type=f32)


def dot_nt(a, b):
    return lax.dot_general(a, b, (((1,), (1,)), ((), ())), preferred_element_type=f32)


def dot_tn(a, b):
    return lax.dot_general(a, b, (((0,), (0,)), ((), ())), preferred_element_type=f32)


def norm_parts(values):
    row_mean = jnp.mean(values, axis=-1, keepdims=True)
    centered = values - row_mean
    row_var = jnp.mean(centered * centered, axis=-1, keepdims=True)
    scale = lax.rsqrt(row_var + NORM_EPS)
    return centered * scale, scale


def norm_back(unit, scale, gain, grad):
    grad_unit = grad * gain
    mean_one = jnp.mean(grad_unit, axis=-1, keepdims=True)
    mean_two = jnp.mean(grad_unit * unit, axis=-1, keepdims=True)
    grad_values = scale * (grad_unit - mean_one - unit * mean_two)
    return grad_values, jnp.sum(grad * unit, axis=0), jnp.sum(grad, axis=0)


def gelu_both(values):
    cubic = GELU_SCALE * (values + 0.044715 * values * values * values)
    tanh = jnp.tanh(cubic)
    half = 0.5 * (1.0 + tanh)
    slope = half + 0.5 * values * (1.0 - tanh * tanh) * GELU_SCALE * (
        1.0 + 3.0 * 0.044715 * values * values
    )
    return values * half, slope


def split_low(values):
    upper = lax.reduce_precision(values, 8, 7)
    return upper.astype(bf16), (values - upper).astype(bf16)


def three_pass(dot, a, b):
    a_up, a_low = split_low(a)
    b_up, b_low = split_low(b)
    return dot(a_up, b_up) + (dot(a_up, b_low) + dot(a_low, b_up))


def product(a, b, exact):
    if exact:
        return three_pass(dot_nn, a, b)
    return dot_nn(a.astype(bf16), b.astype(bf16))


def newton_schulz(rows, gram):
    norm = jnp.sqrt(jnp.trace(gram)) + 1e-07
    rows = rows / norm
    gram = gram / (norm * norm)
    for sweep in range(ITERS):
        exact = sweep in (0, 3, 4)
        square = product(gram, gram, exact)
        poly = POLY_SECOND * gram + POLY_THIRD * square
        rows = POLY_FIRST * rows + product(rows, poly, True)
        if sweep < ITERS - 1:
            half = POLY_FIRST * gram + product(poly, gram, exact)
            gram = POLY_FIRST * half + product(half, poly, exact)
    return rows


MESH = pl.DeviceIdType.MESH
VMEM_SPEC = pl.BlockSpec(memory_space=pltpu.VMEM)
ANY_SPEC = pl.BlockSpec(memory_space=pl.ANY)
HBM_SPEC = pl.BlockSpec(memory_space=pltpu.HBM)
SMEM_SPEC = pl.BlockSpec(memory_space=pltpu.SMEM)
VMEM_BYTES = 60 * 1024 * 1024
VMEM_MUON = 40 * 1024 * 1024
VMEM_FINISH = 36 * 1024 * 1024
ROWS = 16


def place():
    dp = lax.axis_index("dp")
    core = lax.rem(dp, 2)
    chip = lax.div(dp, 2)
    px = lax.rem(chip, 2)
    py = lax.div(chip, 2)
    return dp, core, chip, dp + 1 - 2 * core, dp + 2 - 4 * px, dp + 4 - 8 * py


def push(src, dst, send_sem, recv_sem, target):
    return pltpu.make_async_remote_copy(
        src_ref=src, dst_ref=dst, send_sem=send_sem, recv_sem=recv_sem,
        device_id=target, device_id_type=MESH,
    )


def greet(targets):
    barrier = pltpu.get_barrier_semaphore()
    for target in targets:
        pl.semaphore_signal(barrier, inc=1, device_id=target, device_id_type=MESH)
    pl.semaphore_wait(barrier, len(targets))


def row_splits(row):
    parts = []
    for _ in range(3):
        part = row.astype(bf16)
        parts.append(part.astype(f32))
        row = row - part.astype(f32)
    return jnp.concatenate(parts + [jnp.zeros((5, row.shape[1]), f32)], axis=0).astype(bf16)


def row_repeat(row):
    return jnp.broadcast_to(row, (8, row.shape[1])).astype(bf16)


class PairGather:
    def __init__(self, buf, send, recv, base, near):
        half = buf.shape[1] // 2
        self.copies = {}
        for part in range(2):
            rows = pl.ds(part * half, half)
            for side in range(2):
                index = base + 2 * part + side
                self.copies[side, part] = push(
                    buf.at[0, rows], buf.at[1 + side, rows], send.at[index], recv.at[index],
                    {"dp": near[side]},
                )

    def start(self, part):
        for side in range(2):
            self.copies[side, part].start()

    def wait(self, side, part):
        self.copies[side, part].wait_recv()

    def finish(self):
        for copy in self.copies.values():
            copy.wait_send()


class PairScatter:
    def __init__(self, part, inbox, send, recv, base, near):
        self.half = part.shape[1] // 2
        self.part, self.inbox = part, inbox
        self.copies = {}
        for half in range(2):
            rows = pl.ds(half * self.half, self.half)
            for side in range(2):
                index = base + 2 * half + side
                self.copies[side, half] = push(
                    part.at[side, rows], inbox.at[side, rows], send.at[index], recv.at[index],
                    {"dp": near[side]},
                )

    def put(self, side, half, values):
        self.part[side, pl.ds(half * self.half, self.half)] = values.astype(self.part.dtype)
        self.copies[side, half].start()

    def collect(self, half):
        rows = pl.ds(half * self.half, self.half)
        for side in range(2):
            self.copies[side, half].wait_recv()
        return self.inbox[0, rows].astype(f32) + self.inbox[1, rows].astype(f32)

    def finish(self):
        for copy in self.copies.values():
            copy.wait_send()


class PlaneScatter:
    def __init__(self, part, inbox, send, recv, base, xn, yn):
        self.count = part.shape[0] // 4
        self.half = self.count // 2
        self.part, self.inbox = part, inbox

        def copy(index, source, low, target):
            return push(
                part.at[self.rows(source, low)], inbox.at[index], send.at[base + index],
                recv.at[base + index], {"dp": target},
            )

        self.x_top, self.y_low = copy(0, 1, 0, xn), copy(1, 2, 1, yn)
        self.y_top, self.x_low = copy(2, 2, 0, yn), copy(3, 1, 1, xn)
        self.to_x, self.to_y = copy(4, 3, 0, xn), copy(5, 3, 1, yn)

    def rows(self, slot, low):
        return pl.ds(slot * self.count + low * self.half, self.half)

    def put(self, slot, values):
        self.part[pl.ds(slot * self.count, self.count)] = values.astype(self.part.dtype)
        if slot == 1:
            self.x_top.start()
        elif slot == 2:
            self.y_low.start()
        elif slot == 3:
            self.to_x.start()
            self.to_y.start()

    def add(self, rows, index):
        self.part[rows] = (
            self.part[rows].astype(f32) + self.inbox[index].astype(f32)
        ).astype(self.part.dtype)

    def relay(self):
        self.to_x.wait_recv()
        self.add(self.rows(2, 0), 4)
        self.y_top.start()
        self.to_y.wait_recv()
        self.add(self.rows(1, 1), 5)
        self.x_low.start()

    def collect(self):
        for copy in (self.x_top, self.y_low, self.y_top, self.x_low):
            copy.wait_recv()
        upper = self.inbox[0].astype(f32) + self.inbox[2].astype(f32)
        lower = self.inbox[3].astype(f32) + self.inbox[1].astype(f32)
        own = self.part[pl.ds(0, self.count)].astype(f32)
        return own + jnp.concatenate([upper, lower], axis=0)

    def finish(self):
        for copy in (self.x_top, self.y_low, self.y_top, self.x_low, self.to_x, self.to_y):
            copy.wait_send()


def softmax_half(values):
    values = values * (1.0 / TEMPER)
    shifted = jnp.exp(values - jnp.max(values, axis=-1, keepdims=True))
    return shifted / jnp.sum(shifted, axis=-1, keepdims=True)


class Sems:
    def __init__(self):
        self.used = 0

    def __call__(self, count):
        start = self.used
        self.used += count
        return start


class ShardGather:
    def __init__(self, buf, count, send, recv, sems, peers, sib):
        half = count // 2
        base = sems(6)
        base_sib = sems(4)
        dp, xn, yn, diag = peers
        self.recv_sib = []

        def rows(owner, part):
            start = owner * count + (half if part == 1 else 0)
            return pl.ds(pl.multiple_of(start, 16), count if part == 2 else half)

        def copy(index, owner, part, target):
            area = buf.at[rows(owner, part)]
            return push(area, area, send.at[index], recv.at[index], {"dp": target})

        self.out = [
            copy(base, dp, 0, xn), copy(base + 1, dp, 1, yn),
            copy(base + 2, dp, 1, xn), copy(base + 3, dp, 0, yn),
        ]
        self.into = [
            copy(base, xn, 0, xn), copy(base + 1, yn, 1, yn),
            copy(base + 2, xn, 1, xn), copy(base + 3, yn, 0, yn),
        ]
        self.on = [copy(base + 4, xn, 0, yn), copy(base + 5, yn, 1, xn)]
        self.on_into = [copy(base + 4, diag, 0, yn), copy(base + 5, diag, 1, xn)]
        self.over = [copy(base_sib + i, owner, 2, sib) for i, owner in enumerate(peers)]
        self.over_into = [
            copy(base_sib + i, owner + sib - dp, 2, sib) for i, owner in enumerate(peers)
        ]

    def start(self):
        for item in self.out:
            item.start()
        self.over[0].start()

    def relay(self):
        self.into[0].wait_recv()
        self.on[0].start()
        self.into[1].wait_recv()
        self.on[1].start()

    def cross(self):
        self.into[2].wait_recv()
        self.over[1].start()
        self.into[3].wait_recv()
        self.over[2].start()
        self.on_into[0].wait_recv()
        self.on_into[1].wait_recv()
        self.over[3].start()

    def arrive(self):
        for item in self.over_into:
            item.wait_recv()

    def finish(self):
        for item in self.out + self.on + self.over:
            item.wait_send()


def token_kernel(
    sizes,
    counts_ref, groups_ref, weight_ref, inputs_ref, teacher_ref, w_qkv_ref, w_out_ref,
    w_fc_ref, w_proj_ref, vec_ref,
    out_back_ref, grad_ref, sums_ref, total_ref, centers_ref,
    x_all, teacher_all, full_qkv, full_out, normed, qkv, probs, attended, att_low,
    fc_sets, proj_sets, wide_buf, tokens, active, slope, grad_y_all,
    grad_gate, part_ffn, inbox_ffn, means, fc_grads, proj_grads,
    swap_ffn, ffn_from, ffn_sum, chain_in, att_grad, grad_mixed, qkv_grads, out_grads, swap_att,
    inbox_att, att_sum, plane_in, rows_own, rows_in, rows_plane, load_sems, send, recv,
):
    width = vec_ref.shape[1]
    blocks, positions = inputs_ref.shape[:2]
    length = blocks * positions
    units = w_proj_ref.shape[0]
    n_qkv, n_out = w_qkv_ref.shape[0], w_out_ref.shape[0]
    dp, core, chip, sib, xn, yn = place()
    diag = xn + yn - dp
    peers = (dp, xn, yn, diag)
    z = lax.axis_index("blk")
    planes = lax.axis_size("blk")
    ranks = lax.axis_size("dp")
    root = z == 0
    near = (jnp.where(core == 0, yn, xn), jnp.where(core == 0, xn, yn))
    weight_near = near[1]
    near_chips = tuple(lax.div(item, 2) for item in near)
    to_sib = {"dp": sib}
    sems = Sems()

    def turn(k):
        return lax.rem(dp + k, ranks)

    def plane(k):
        return lax.rem(z + k, planes)

    def total(values):
        return jnp.sum(values, axis=0, keepdims=True)

    sharers = (
        [(0, {"dp": dp, "blk": plane(k)}) for k in range(1, planes)]
        + [(1, {"dp": sib, "blk": plane(k)}) for k in range(planes)]
        + [(2, {"dp": weight_near, "blk": plane(k)}) for k in range(planes)]
        + [(3, {"dp": weight_near + sib - dp, "blk": plane(k)}) for k in range(planes)]
    )
    far = [item for item in (near[0], near[0] + sib - dp, diag, diag + sib - dp)]
    greet([target for _, target in sharers] + [{"dp": item} for item in far])
    hidden_buf, grad_y = wide_buf.at[pl.ds(0, length)], wide_buf.at[pl.ds(length, length)]
    fc_load = pltpu.make_async_copy(
        w_fc_ref, slope.at[pl.ds(0, w_fc_ref.shape[0])], load_sems.at[0]
    )
    proj_load = pltpu.make_async_copy(w_proj_ref, wide_buf.at[pl.ds(0, units)], load_sems.at[1])
    fc_load.start()
    proj_load.start()

    full_qkv[pl.ds(pl.multiple_of(dp * n_qkv, 16), n_qkv)] = w_qkv_ref[...].astype(bf16)
    gather_qkv = ShardGather(full_qkv, n_qkv, send, recv, sems, peers, sib)
    gather_qkv.start()

    def token_exchange(source, target):
        at = sems(8)
        sends, waits = [], []
        for k in range(1, planes):
            other = plane(k)
            sends.append(
                push(
                    source.at[other], target.at[z], send.at[at + k], recv.at[at + z],
                    {"blk": other},
                )
            )
            waits.append(
                push(
                    source.at[other], target.at[other], send.at[at + k], recv.at[at + other],
                    {"blk": other},
                )
            )
        return sends, waits

    inputs_out, inputs_in = token_exchange(inputs_ref, x_all)
    teacher_out, teacher_in = token_exchange(teacher_ref, teacher_all)
    for copy in inputs_out:
        copy.start()
    x_all[z] = inputs_ref[z]
    full_out[pl.ds(pl.multiple_of(dp * n_out, 16), n_out)] = w_out_ref[...].astype(bf16)
    gather_out = ShardGather(full_out, n_out, send, recv, sems, peers, sib)
    fc_load.wait()
    proj_load.wait()
    fc_sets[0, 0] = slope[: w_fc_ref.shape[0]].astype(bf16).T
    proj_sets[0, 0] = wide_buf[:units].astype(bf16)
    at = sems(6)

    def weight_push(ref, source, goal, index, target):
        return push(ref.at[source], ref.at[goal], send.at[index], recv.at[index], {"dp": target})

    weights_sib, weights_near, weights_on = [
        [
            weight_push(ref, source, goal, at + 2 * i + j, target)
            for j, ref in enumerate((fc_sets, proj_sets))
        ]
        for i, (source, goal, target) in enumerate(
            (((0, 0), (1, 0), sib), ((0, 0), (0, 1), weight_near), ((0, 1), (1, 1), sib))
        )
    ]
    for copy in weights_sib + teacher_out:
        copy.start()
    teacher_all[z] = teacher_ref[z]

    gather_qkv.relay()
    gather_out.start()
    for copy in inputs_in:
        copy.wait_recv()
    x = x_all[...].reshape(length, width).astype(f32)
    unit_one, _ = norm_parts(x)
    center_one = vec_ref[1:2].astype(bf16).astype(f32)
    low_normed = (unit_one * vec_ref[0:1] + vec_ref[1:2]).astype(bf16)
    normed[...] = (unit_one * vec_ref[0:1] + (vec_ref[1:2] - center_one)).astype(bf16)
    gather_qkv.cross()
    gather_out.relay()
    for copy in weights_near:
        copy.start()
    gather_qkv.arrive()

    for part, bias in ((0, vec_ref[2:3]), (1, None), (2, vec_ref[3:4])):
        values = dot_nt(low_normed, full_qkv[part * width : (part + 1) * width])
        qkv[part] = (values if bias is None else values + bias).astype(bf16)
    center_out = (
        dot_nt(row_repeat(center_one), full_qkv[2 * width :])[0:1] + vec_ref[3:4]
    ).astype(bf16).astype(f32)

    pair_width = 2 * HD
    pair_count = H // 2
    lane = lax.broadcasted_iota(jnp.int32, (length, pair_width), 1)
    sides = (lane < HD, lane >= HD)
    visible = lax.broadcasted_iota(jnp.int32, (length, length), 1) <= lax.broadcasted_iota(
        jnp.int32, (length, length), 0
    )

    def only(values, side):
        return jnp.where(sides[side], values, jnp.zeros_like(values))

    @pl.loop(0, pair_count, unroll=3)
    def _(pair):
        lanes = pl.ds(pl.multiple_of(pair * pair_width, pair_width), pair_width)
        queries, keys, values = qkv[0, :, lanes], qkv[1, :, lanes], qkv[2, :, lanes]
        both = []
        for side in range(2):
            scores = dot_nt(only(queries, side), keys) * 0.125
            scores = jnp.where(visible, scores, MASKED)
            weights = jnp.exp(scores - jnp.max(scores, axis=-1, keepdims=True))
            weights = weights * (1.0 / jnp.sum(weights, axis=-1, keepdims=True))
            probs[2 * pair + side] = weights
            both.append(dot_nn(weights.astype(bf16), values))
        result = jnp.where(sides[0], both[0], both[1])
        attended[:, lanes] = result
        att_low[:, lanes] = result.astype(bf16)

    gather_out.cross()
    gather_out.arrive()
    hidden = x + dot_nt(att_low[...], full_out[...]) + vec_ref[4:5]
    hidden_buf[...] = hidden
    att_low[...] = (attended[...] - center_out).astype(bf16)

    gather = PairGather(tokens, send, recv, sems(4), near)
    half = length // 2
    for part in range(2):
        unit_two, _ = norm_parts(hidden[part * half : (part + 1) * half])
        tokens[0, pl.ds(part * half, half)] = (
            unit_two * vec_ref[5:6] + vec_ref[6:7]
        ).astype(bf16)
        gather.start(part)
    for copy in weights_near:
        copy.wait_recv()
    for copy in weights_on:
        copy.start()

    def by_core(row):
        low_row, high_row = row[:, :units], row[:, units:]
        return (
            jnp.where(core == 0, low_row, high_row), jnp.where(core == 0, high_row, low_row)
        )

    def bias_of(item):
        return by_core(vec_ref[pl.ds(7 + item, 1), :])

    own_bias = bias_of(chip)
    bias = (
        (own_bias[0], bias_of(near_chips[1])[0]), (own_bias[1], bias_of(near_chips[0])[1])
    )
    pieces = [(side, part) for part in range(2) for side in range(2)]

    def place_of(side, which, slot):
        return (4 * side + 2 * which + slot) * length

    def forward(side, slot, start, size):
        block = 0 if slot == 0 else 1 + side
        result = None
        for which in range(2):
            gate_in = dot_nt(
                tokens[block, pl.ds(start, size)], fc_sets[side, which]
            ) + bias[side][which]
            value, rate = gelu_both(gate_in)
            value = value.astype(bf16)
            rows = pl.ds(place_of(side, which, slot) + start, size)
            active[rows] = value
            slope[rows] = rate
            value = dot_nn(value, proj_sets[side, which])
            result = value if result is None else result + value
        return result

    scatter = PairScatter(part_ffn, inbox_ffn, send, recv, sems(4), near)
    own_part = forward(0, 0, 0, length)
    for copy in weights_sib + weights_on:
        copy.wait_recv()
    own_part = own_part + forward(1, 0, 0, length)
    for side, part in pieces:
        gather.wait(side, part)
        scatter.put(side, part, forward(side, 1, part * half, half))

    count = 2 * length
    mean_at = sems(len(sharers))
    to_sharers = [
        push(means.at[0], means.at[number], send.at[mean_at + k], recv.at[mean_at + number], target)
        for k, (number, target) in enumerate(sharers)
    ]
    mean_waits = [
        push(means.at[0], means.at[number], send.at[mean_at], recv.at[mean_at + number], to_sib)
        for number in range(4)
    ]

    @pl.when(root)
    def _():
        means[0] = jnp.zeros(means.shape[1:], f32)
        token_sum = total(tokens[0].astype(f32)) + total(tokens[1].astype(f32))
        unit_sum = total(active[pl.ds(place_of(0, 0, 0), count)].astype(f32))
        means[0, 0:1] = (token_sum * (1.0 / count)).astype(bf16).astype(f32)
        means[0, 1:2, :units] = (unit_sum * (1.0 / count)).astype(bf16).astype(f32)
        for copy in to_sharers:
            copy.start()

    for copy in teacher_in:
        copy.wait_recv()
    target = softmax_half(teacher_all[...].reshape(length, width).astype(f32))
    group = groups_ref[z]
    seq_weight = jnp.where(z < counts_ref[0], weight_ref[group], 0.0)
    out_low = teacher_all
    gather_two = PairGather(grad_y_all, send, recv, sems(4), near)
    half_blocks = blocks // 2
    for part in range(2):
        rows = slice(part * half, (part + 1) * half)
        block_out = hidden_buf[rows] + own_part[rows] + vec_ref[11:12] + scatter.collect(part)
        own_grad_y = (seq_weight * (width / TEMPER)) * (softmax_half(block_out) - target[rows])
        grad_y[rows] = own_grad_y
        grad_y_all[0, pl.ds(part * half, half)] = own_grad_y.astype(bf16)
        gather_two.start(part)
        out_low[pl.ds(part * half_blocks, half_blocks)] = block_out.astype(bf16).reshape(
            half_blocks, positions, width
        )
    back_out, back_in = token_exchange(out_low, out_back_ref)
    for copy in back_out:
        copy.start()
    out_back_ref[z] = out_low[z]

    def backward(side, slot, start, size):
        block = 0 if slot == 0 else 1 + side
        result = None
        for which in range(2):
            rows = pl.ds(place_of(side, which, slot) + start, size)
            grad_active = dot_nt(grad_y_all[block, pl.ds(start, size)], proj_sets[side, which])
            value = (grad_active * slope[rows]).astype(bf16)
            grad_gate[rows] = value
            value = dot_nn(value, fc_sets[side, which])
            result = value if result is None else result + value
        return result

    scatter.finish()
    scatter_two = PairScatter(part_ffn, inbox_ffn, send, recv, sems(4), near)
    own_part = backward(0, 0, 0, length) + backward(1, 0, 0, length)
    for side, part in pieces:
        gather_two.wait(side, part)
        scatter_two.put(side, part, backward(side, 1, part * half, half))

    @pl.when(jnp.logical_not(root))
    def _():
        mean_waits[0].wait_recv()

    for copy in mean_waits[1:]:
        copy.wait_recv()

    plane_at, chunk_at = sems(16), sems(16)

    def plane_source(goal, chunk=0):
        if goal == 2:
            return att_sum.at[pl.ds(n_qkv, n_out)]
        return att_sum.at[pl.ds(chunk * n_out, n_out)]

    def plane_copy(source, goal, chunk=0):
        if goal == 1:
            index = chunk_at + 4 * source + chunk
            rows = pl.ds(chunk * n_out, n_out)
            if source == 3:
                return push(
                    plane_source(goal, chunk), chain_in.at[1, rows], send.at[index],
                    recv.at[index], {"blk": 2},
                )
        else:
            index = plane_at + 4 * source + goal
            rows = pl.ds(0, sizes[goal])
        return push(
            plane_source(goal, chunk), plane_in.at[(source - goal) % 4 - 1, rows], send.at[index],
            recv.at[index], {"blk": goal},
        )

    chunk_count = n_qkv // n_out

    def send_plane(goal, chunk=0):
        for source in range(4):
            if source != goal and (goal, source) != (1, 2):
                @pl.when(z == source)
                def _():
                    plane_copy(source, goal, chunk).start()

    def add_chunk(chunk):
        @pl.when(z == 2)
        def _():
            plane_copy(3, 1, chunk).wait_recv()
            rows = pl.ds(chunk * n_out, n_out)
            att_sum[rows] = (
                att_sum[rows].astype(f32) + chain_in[1, rows].astype(f32)
            ).astype(bf16)
            plane_copy(2, 1, chunk).start()

    at = sems(4)
    ffn_swap, ffn_near = [], []
    for i, (grads, held) in enumerate(((fc_grads, fc_sets), (proj_grads, proj_sets))):
        ffn_swap.append(
            push(grads.at[1], swap_ffn.at[i], send.at[at + i], recv.at[at + i], to_sib)
        )
        ffn_near.append(
            push(
                held.at[1, 0], ffn_from.at[i], send.at[at + 2 + i], recv.at[at + 2 + i],
                {"dp": weight_near},
            )
        )

    def pass_ffn(i):
        ffn_swap[i].wait_recv()
        grads, held = ((fc_grads, fc_sets), (proj_grads, proj_sets))[i]
        held[1, 0] = (grads[0, 1].astype(f32) + swap_ffn[i, 1].astype(f32)).astype(bf16)
        ffn_near[i].start()

    chain_at = sems(4)
    far_plane, add_plane, near_plane, goal_plane = (0, 3), (1, 2), (2, 1), (3, 0)

    def chain_copy(i, source):
        slot = 1 if source == add_plane[i] else 0
        goal = add_plane[i] if source == far_plane[i] else goal_plane[i]
        number = chain_at + 2 * i + slot
        return push(
            ffn_sum.at[i], chain_in.at[slot], send.at[number], recv.at[number], {"blk": goal}
        )

    def first_hop(i):
        @pl.when(jnp.logical_or(z == far_plane[i], z == near_plane[i]))
        def _():
            @pl.when(z == far_plane[i])
            def _():
                chain_copy(i, far_plane[i]).start()

            @pl.when(z == near_plane[i])
            def _():
                chain_copy(i, near_plane[i]).start()

    def second_hop(i):
        @pl.when(z == add_plane[i])
        def _():
            chain_copy(i, far_plane[i]).wait_recv()
            ffn_sum[i] = (ffn_sum[i].astype(f32) + chain_in[0].astype(f32)).astype(bf16)
            chain_copy(i, add_plane[i]).start()

    def sum_ffn(i):
        ffn_near[i].wait_recv()
        grads = (fc_grads, proj_grads)[i]
        ffn_sum[i] = (
            grads[0, 0].astype(f32) + swap_ffn[i, 0].astype(f32) + ffn_from[i].astype(f32)
        ).astype(bf16)
        first_hop(i)

    def shard_rows(ref, side, which):
        return ref[pl.ds(place_of(side, which, 0), count)]

    def both_blocks(ref, side):
        return jnp.concatenate([ref[0], ref[1 + side]], axis=0)

    gate_sums = {}

    def proj_side(side):
        grads = both_blocks(grad_y_all, side)
        for which in range(2):
            center = means[2 * which + side, 1:2, :units]
            values = (shard_rows(active, side, which).astype(f32) - center).astype(bf16)
            proj_grads[side, which] = dot_tn(values, grads).astype(bf16)

    def fc_side(side):
        block = both_blocks(tokens, side).astype(f32)
        for which in range(2):
            gate = shard_rows(grad_gate, side, which)
            gate_sums[side, which] = total(gate.astype(f32))
            center = means[2 * which + side, 0:1]
            fc_grads[side, which] = dot_tn(gate, (block - center).astype(bf16)).astype(bf16)

    proj_side(1)
    ffn_swap[1].start()
    proj_side(0)
    fc_side(1)
    ffn_swap[0].start()
    pass_ffn(1)
    fc_side(0)

    grad_normed = own_part + jnp.concatenate(
        [scatter_two.collect(0), scatter_two.collect(1)], axis=0
    )
    own_grad_y = grad_y[...]
    unit_two, scale_two = norm_parts(hidden_buf[...])
    back, gain_row, shift_row = norm_back(unit_two, scale_two, vec_ref[5:6], grad_normed)
    grad_hidden = own_grad_y + back
    low_hidden = grad_hidden.astype(bf16)
    hidden_sum = total(low_hidden.astype(f32))
    pass_ffn(0)
    rows_own[...] = jnp.zeros_like(rows_own)
    rows_own[4:5] = total(grad_hidden)
    rows_own[5:6] = gain_row[None]
    rows_own[6:7] = shift_row[None]
    blank = jnp.zeros((1, units), f32)

    def in_order(first, second):
        return jnp.where(
            core == 0,
            jnp.concatenate([first, second], axis=1),
            jnp.concatenate([second, first], axis=1),
        )

    rows_own[pl.ds(7 + chip, 1), :] = in_order(gate_sums[0, 0], gate_sums[1, 0])
    rows_own[pl.ds(7 + near_chips[1], 1), :] = in_order(gate_sums[0, 1], blank)
    rows_own[pl.ds(7 + near_chips[0], 1), :] = in_order(blank, gate_sums[1, 1])
    rows_own[11:12] = total(own_grad_y)
    rows_own[14:15] = total(own_grad_y.astype(bf16).astype(f32))
    grad_y[...] = grad_hidden

    out_grads[...] = dot_tn(low_hidden, att_low[...]).astype(bf16)
    at_swap = sems(16)

    def swap_copy(chunk, slot):
        owner = peers[slot] + 1 - 2 * core
        if chunk == 0:
            source = out_grads.at[pl.ds(pl.multiple_of(owner * n_out, 16), n_out)]
        else:
            start = owner * n_qkv + (chunk - 1) * n_out
            source = qkv_grads.at[pl.ds(pl.multiple_of(start, 16), n_out)]
        index = at_swap + 4 * chunk + slot
        return push(source, swap_att.at[chunk, slot], send.at[index], recv.at[index], to_sib)

    def own_rows(chunk, slot):
        if chunk == 0:
            return out_grads[pl.ds(pl.multiple_of(peers[slot] * n_out, 16), n_out)]
        start = peers[slot] * n_qkv + (chunk - 1) * n_out
        return qkv_grads[pl.ds(pl.multiple_of(start, 16), n_out)]

    swaps = [[swap_copy(chunk, slot) for slot in range(4)] for chunk in range(chunk_count + 1)]
    scatters = [
        PlaneScatter(proj_grads.at[c // 2, c % 2], inbox_att.at[c], send, recv, sems(6), xn, yn)
        for c in range(chunk_count + 1)
    ]

    def start_swap(chunk):
        for slot in (3, 2, 1, 0):
            swaps[chunk][slot].start()

    def put_chunk(chunk):
        for slot in (3, 2, 1, 0):
            swaps[chunk][slot].wait_recv()
            scatters[chunk].put(
                slot,
                own_rows(chunk, slot).astype(f32) + swap_att[chunk, slot].astype(f32),
            )

    def collect_chunk(chunk):
        rows = pl.ds(n_qkv if chunk == 0 else (chunk - 1) * n_out, n_out)
        att_sum[rows] = scatters[chunk].collect().astype(bf16)
        send_plane(2 if chunk == 0 else 1, max(chunk - 1, 0))

    start_swap(0)
    sum_ffn(1)
    ffn_swap[1].wait_send()
    grad_att = dot_nn(low_hidden, full_out[...]).astype(bf16)
    att_grad[...] = grad_att
    put_chunk(0)

    def pair_backward(pair):
        lanes = pl.ds(pl.multiple_of(pair * pair_width, pair_width), pair_width)
        queries, keys, values = qkv[0, :, lanes], qkv[1, :, lanes], qkv[2, :, lanes]
        grads = att_grad[:, lanes]
        product = grads.astype(f32) * attended[:, lanes]
        found = []
        for side in range(2):
            weights = probs[2 * pair + side]
            delta = jnp.sum(only(product, side), axis=-1, keepdims=True)
            grad_probs = dot_nt(only(grads, side), values)
            grad_scores = (weights * (grad_probs - delta)).astype(bf16)
            found.append(
                (
                    dot_nn(grad_scores, keys) * 0.125,
                    dot_tn(grad_scores, queries) * 0.125,
                    dot_tn(weights.astype(bf16), grads),
                )
            )
        for part in range(3):
            start = pl.multiple_of(part * width + pair * pair_width, pair_width)
            grad_mixed[:, pl.ds(start, pair_width)] = jnp.where(
                sides[0], found[0][part], found[1][part]
            ).astype(bf16)

    pl.loop(0, 2, unroll=2)(pair_backward)
    sum_ffn(0)
    pl.loop(2, pair_count, unroll=4)(pair_backward)
    scatters[0].relay()
    second_hop(1)
    mixed_sum = total(grad_mixed[...].astype(f32))
    strip = width // 2

    @pl.loop(0, full_qkv.shape[0] // strip, unroll=2)
    def _(step):
        rows = pl.ds(pl.multiple_of(step * strip, strip), strip)
        qkv_grads[rows] = dot_tn(grad_mixed[:, rows], normed[...]).astype(bf16)

    for chunk in range(1, chunk_count + 1):
        start_swap(chunk)
    collect_chunk(0)
    for chunk in range(1, chunk_count + 1):
        put_chunk(chunk)

    grad_one = dot_nn(grad_mixed[...], full_qkv[...])
    scatters[1].relay()
    second_hop(0)
    unit_one, scale_one = norm_parts(x_all[...].reshape(length, width).astype(f32))
    back, gain_row, shift_row = norm_back(unit_one, scale_one, vec_ref[0:1], grad_one)
    grad_ref[...] = (grad_y[...] + back).astype(bf16).reshape(grad_ref.shape)
    scatters[2].relay()
    collect_chunk(1)
    rows_own[0:1] = gain_row[None]
    rows_own[1:2] = shift_row[None]
    rows_own[2:3] = mixed_sum[:, :width]
    rows_own[3:4] = mixed_sum[:, 2 * width :]
    for rank in range(8):
        rows_own[16 + rank : 17 + rank, :n_qkv] = mixed_sum[:, rank * n_qkv : (rank + 1) * n_qkv]
        rows_own[16 + rank : 17 + rank, units : units + n_out] = hidden_sum[
            :, rank * n_out : (rank + 1) * n_out
        ]

    at = sems(8)
    row_sends, row_waits = [], []
    for k in range(1, ranks):
        row_sends.append(
            push(rows_own, rows_in.at[dp], send.at[at + k], recv.at[at + dp], {"dp": turn(k)})
        )
        source = turn(k)
        row_waits.append(
            push(rows_own, rows_in.at[source], send.at[at + k], recv.at[at + source], to_sib)
        )
        row_sends[-1].start()
    rows_in[dp] = rows_own[...]
    scatters[3].relay()
    collect_chunk(2)
    add_chunk(0)
    for copy in row_waits:
        copy.wait_recv()
    rows_sum = rows_in[0]
    for k in range(1, ranks):
        rows_sum = rows_sum + rows_in[k]
    rows_plane[z] = rows_sum
    plane_rows, plane_rows_in = token_exchange_rows(rows_plane, z, plane, planes, sems, send, recv)
    for copy in plane_rows:
        copy.start()
    add_chunk(1)
    collect_chunk(3)
    for copy in plane_rows_in:
        copy.wait_recv()
    every_row = rows_plane[0]
    for k in range(1, planes):
        every_row = every_row + rows_plane[k]
    total_ref[...] = every_row
    add_chunk(2)
    centers_ref[...] = means[0]
    centers_ref[2:3] = center_one
    centers_ref[3:4] = center_out

    for goal in range(4):
        @pl.when(z == goal)
        def _():
            size = sizes[goal]
            if goal in (0, 3):
                i = 1 - goal // 3
                for source in (near_plane[i], add_plane[i]):
                    chain_copy(i, source).wait_recv()
                value = ffn_sum[i].astype(f32) + (
                    chain_in[0].astype(f32) + chain_in[1].astype(f32)
                )
            else:
                value = (att_sum[:n_qkv] if goal == 1 else att_sum[n_qkv:]).astype(f32)
                for source in range(4):
                    if source == goal:
                        continue
                    if (goal, source) == (1, 3):
                        continue
                    for chunk in range(chunk_count if goal == 1 else 1):
                        plane_copy(source, goal, chunk).wait_recv()
                    slot = (source - goal) % 4 - 1
                    value = value + plane_in[slot, :size].astype(f32)
            if size < units:
                sums_ref[size:] = jnp.zeros((units - size, width), bf16)
            sums_ref[:size] = value.astype(bf16)
            for other in (1, 2):
                if other != goal:
                    for chunk in range(chunk_count if other == 1 else 1):
                        plane_copy(goal, other, chunk).wait_send()
            for i in range(2):
                if goal != goal_plane[i]:
                    chain_copy(i, goal).wait_send()

    for copy in back_in:
        copy.wait_recv()
    for copy in (
        inputs_out + teacher_out + weights_sib + weights_near + weights_on + back_out + ffn_swap[:1]
        + ffn_near + row_sends + plane_rows
        + [copy for chunk in swaps for copy in chunk]
    ):
        copy.wait_send()
    for item in (gather_qkv, gather_out, gather, gather_two, scatter_two, *scatters):
        item.finish()

    @pl.when(root)
    def _():
        for copy in to_sharers:
            copy.wait_send()


def token_exchange_rows(ref, z, plane, planes, sems, send, recv):
    at = sems(8)
    sends, waits = [], []
    for k in range(1, planes):
        other = plane(k)
        sends.append(
            push(ref.at[z], ref.at[z], send.at[at + k], recv.at[at + z], {"blk": other})
        )
        waits.append(
            push(ref.at[other], ref.at[other], send.at[at + k], recv.at[at + other], {"blk": other})
        )
    return sends, waits


def token_pass(counts, groups, group_weight, inputs, teacher, w_qkv, w_out, w_fc, w_proj, vectors):
    blocks, positions, width = inputs.shape
    length = blocks * positions
    n_qkv, n_out, units = w_qkv.shape[0], w_out.shape[0], w_proj.shape[0]
    chunks = 1 + n_qkv // n_out
    tokens = pltpu.VMEM((3, length, width), bf16)
    pair = pltpu.VMEM((2, length, width), bf16)
    low_rows = pltpu.VMEM((units, width), bf16)
    two_rows = pltpu.VMEM((2, units, width), bf16)
    four_rows = pltpu.VMEM((2, 2, units, width), bf16)
    unit_rows = 8 * length
    row_count = 24
    back = jax.ShapeDtypeStruct((blocks, positions, width), bf16)
    return pl.pallas_call(
        functools.partial(token_kernel, (units, n_qkv, n_out, units)),
        out_shape=(
            back, back,
            jax.ShapeDtypeStruct((units, width), bf16),
            jax.ShapeDtypeStruct((row_count, width), f32),
            jax.ShapeDtypeStruct((8, width), f32),
        ),
        in_specs=[SMEM_SPEC] * 3 + [VMEM_SPEC] * 4 + [ANY_SPEC] * 2 + [VMEM_SPEC],
        out_specs=(VMEM_SPEC,) * 5,
        scratch_shapes=[
            pltpu.VMEM((blocks, positions, width), bf16),
            pltpu.VMEM((blocks, positions, width), bf16),
            pltpu.VMEM((8 * n_qkv, width), bf16),
            pltpu.VMEM((8 * n_out, width), bf16),
            pltpu.VMEM((length, width), bf16),
            pltpu.VMEM((3, length, width), bf16),
            pltpu.VMEM((H, length, length), f32),
            pltpu.VMEM((length, width), f32),
            pltpu.VMEM((length, width), bf16),
            four_rows, four_rows,
            pltpu.VMEM((2 * length, width), f32),
            tokens,
            pltpu.VMEM((unit_rows, units), bf16),
            pltpu.VMEM((unit_rows, units), f32),
            tokens,
            pltpu.VMEM((unit_rows, units), bf16),
            pair, pair,
            pltpu.VMEM((4, 8, width), f32),
            four_rows, four_rows, four_rows, two_rows, two_rows, two_rows,
            pltpu.VMEM((length, width), bf16),
            pltpu.VMEM((length, 3 * width), bf16),
            pltpu.VMEM((8 * n_qkv, width), bf16),
            pltpu.VMEM((8 * n_out, width), bf16),
            pltpu.VMEM((chunks, 4, n_out, width), bf16),
            pltpu.VMEM((chunks, 6, n_out // 2, width), bf16),
            low_rows,
            pltpu.VMEM((3, n_qkv, width), bf16),
            pltpu.VMEM((row_count, width), f32),
            pltpu.VMEM((8, row_count, width), f32),
            pltpu.VMEM((4, row_count, width), f32),
            pltpu.SemaphoreType.DMA((2,)),
            pltpu.SemaphoreType.DMA((220,)),
            pltpu.SemaphoreType.DMA((220,)),
        ],
        compiler_params=pltpu.CompilerParams(
            collective_id=0, has_side_effects=True, vmem_limit_bytes=VMEM_BYTES
        ),
        name="tokens",
    )(counts, groups, group_weight, inputs, teacher, w_qkv, w_out, w_fc, w_proj, vectors)


def split_pair(values):
    upper = values.astype(bf16)
    return upper, (values - upper.astype(f32)).astype(bf16)


class Chain:
    def __init__(self, ref, sizes, send, recv, sems):
        self.ref, self.sizes, self.send, self.recv = ref, sizes, send, recv
        self.begin = (sems(32), sems(32))
        self.arrivals = [[] for _ in sizes]
        planes = len(sizes)
        for way in range(2):
            ahead = 1 if way == 0 else -1
            plane = 0 if way == 0 else planes - 1
            passing = []
            while 0 <= plane + ahead < planes:
                queue = [(0.0, plane, index) for index in range(self.chunks(plane))] + passing
                clock, passing = 0.0, []
                for ready, source, index in sorted(queue):
                    clock = max(clock, ready) + sizes[source] / self.chunks(source)
                    passing.append((clock + 32.0, source, index))
                plane += ahead
                self.arrivals[plane] += [(*item, way) for item in passing]
        for item in self.arrivals:
            item.sort()

    def chunks(self, source):
        return 2 if self.sizes[source] <= 96 else 6

    def move(self, source, index, goal, way):
        rows_each = self.sizes[source] // self.chunks(source)
        area = self.ref.at[source, pl.ds(index * rows_each, rows_each)]
        number = self.begin[way] + 8 * source + index
        return push(area, area, self.send.at[number], self.recv.at[number], {"blk": goal})

    def onward(self, plane, way):
        goal = plane + (1 if way == 0 else -1)
        return goal if 0 <= goal < len(self.sizes) else None

    def start(self, plane, index):
        if index < self.chunks(plane):
            for way in range(2):
                goal = self.onward(plane, way)
                if goal is not None:
                    self.move(plane, index, goal, way).start()

    def hop(self, plane, first, last):
        count = len(self.arrivals[plane])
        for _, source, index, way in self.arrivals[plane][count * first // 4 : count * last // 4]:
            self.move(source, index, plane, way).wait_recv()
            goal = self.onward(plane, way)
            if goal is not None:
                self.move(source, index, goal, way).start()

    def finish(self, plane):
        own = [(0.0, plane, index, way) for index in range(self.chunks(plane)) for way in range(2)]
        for _, source, index, way in own + self.arrivals[plane]:
            goal = self.onward(plane, way)
            if goal is not None:
                self.move(source, index, goal, way).wait_send()


def muon_kernel(
    sizes,
    own_ref, total_in_ref, centers_in_ref, grad_ref,
    mom_proj_ref, mom_qkv_ref, mom_out_ref, mom_fc_ref,
    sums_ref, update_ref, grad_back_ref,
    total_ref, centers_ref, small_sems,
    gram_own, gram_other, gram_swap, gram_in, gram_all,
    gram, gram_up, gram_low, poly_up, poly_low, half, half_up, half_low,
    iterate, iter_up, iter_low, mom_wide, mom_rows, mom_sems, send, recv,
):
    units, width = own_ref.shape
    dp, core, chip, sib, xn, yn = place()
    z = lax.axis_index("blk")
    planes = lax.axis_size("blk")
    small_in = [
        pltpu.make_async_copy(source, target, small_sems.at[i])
        for i, (source, target) in enumerate(
            (
                (own_ref, sums_ref.at[z]), (total_in_ref, total_ref),
                (centers_in_ref, centers_ref), (grad_ref.at[z], grad_back_ref.at[z]),
            )
        )
    ]
    for copy in small_in:
        copy.start()
    diag = xn + yn - dp
    peers = (dp, xn, yn, diag)
    to_sib = {"dp": sib}
    sems = Sems()

    def each_plane(action):
        for plane in range(4):
            @pl.when(z == plane)
            def _():
                action(plane)

    mom_in = (
        (mom_proj_ref, mom_rows),
        (mom_qkv_ref, mom_rows.at[pl.ds(0, sizes[1])]),
        (mom_out_ref, mom_rows.at[pl.ds(0, sizes[2])]),
        (mom_fc_ref, mom_wide),
    )

    def load_momentum(plane):
        pltpu.make_async_copy(*mom_in[plane], mom_sems.at[plane]).start()

    def take_momentum(plane):
        pltpu.make_async_copy(*mom_in[plane], mom_sems.at[plane]).wait()
        if plane == 3:
            mom_rows[...] = mom_wide[...].T
        if sizes[plane] < units:
            mom_rows[sizes[plane] :] = jnp.zeros((units - sizes[plane], width), f32)

    each_plane(load_momentum)
    greet(
        [to_sib, {"dp": xn}, {"dp": yn}, {"dp": diag}]
        + [{"blk": lax.rem(z + k, planes)} for k in range(1, planes)]
    )
    small_in[0].wait()
    sums_chain = Chain(sums_ref, sizes, send, recv, sems)
    each_plane(lambda plane: [sums_chain.start(plane, index) for index in range(6)])
    at = sems(8)
    back_out, back_in = [], []
    for k in range(1, planes):
        other = lax.rem(z + k, planes)
        back_out.append(
            push(
                grad_ref.at[other], grad_back_ref.at[z], send.at[at + k], recv.at[at + z],
                {"blk": other},
            )
        )
        back_in.append(
            push(
                grad_ref.at[other], grad_back_ref.at[other], send.at[at + k],
                recv.at[at + other], {"blk": other},
            )
        )
        back_out[-1].start()
    for copy in small_in[1:]:
        copy.wait()
    own_total = total_ref[pl.ds(16 + dp, 1), :]
    gate_row = total_ref[pl.ds(7 + chip, 1), :]

    def by_core(row):
        return jnp.where(core == 0, row[:, :units], row[:, units:])

    sum_row = jnp.where(
        z == 3, by_core(gate_row), jnp.where(z == 1, own_total[:, :units], own_total[:, units:])
    )
    mean_row = jnp.where(
        z == 3, centers_ref[0:1], jnp.where(z == 1, centers_ref[2:3], centers_ref[3:4])
    )
    left = jnp.where(
        z == 0,
        jnp.broadcast_to(centers_ref[1:2, :units], (8, units)),
        row_splits(sum_row).astype(f32),
    ).astype(bf16)
    right = jnp.where(
        z == 0,
        row_splits(total_ref[14:15]).astype(f32),
        jnp.broadcast_to(mean_row, (8, width)),
    ).astype(bf16)
    each_plane(take_momentum)
    value = MOMENT_DECAY * mom_rows[...] + (sums_ref[z].astype(f32) + dot_tn(left, right))
    iterate[...] = value
    value_up, value_low = split_pair(value)
    iter_up[...] = value_up
    iter_low[...] = value_low

    tile = gram_own.shape[1]
    quarter = tile // 4
    pairs = [(0, 0), (0, 1), (0, 2), (1, 1), (1, 2), (2, 2)]

    def gram_block(side, index):
        (i, j), (k, l) = pairs[index], pairs[3 + index]
        first = pl.ds(pl.multiple_of(jnp.where(side == 0, i, k) * tile, tile), tile)
        second = pl.ds(pl.multiple_of(jnp.where(side == 0, j, l) * tile, tile), tile)
        upper, lower = iter_up[:, first], iter_low[:, first]
        return dot_tn(
            jnp.concatenate([upper, upper, lower], axis=0),
            jnp.concatenate([iter_up[:, second], iter_low[:, second], iter_up[:, second]], axis=0),
        )

    at = sems(3)
    gram_sib = [
        push(gram_other.at[k], gram_swap.at[k], send.at[at + k], recv.at[at + k], to_sib)
        for k in range(3)
    ]
    for k in range(3):
        gram_other[k] = gram_block(1 - core, k)
        gram_sib[k].start()
    others = (chip, lax.div(xn, 2), lax.div(yn, 2), lax.div(diag, 2))
    at = sems(12)

    def quarter_of(item):
        return pl.ds(pl.multiple_of(item * quarter, quarter), quarter)

    gram_sends = []
    for k in range(3):
        gram_own[k] = gram_block(core, k)
    for k in range(3):
        gram_sib[k].wait_recv()
        gram_own[k] = gram_own[k] + gram_swap[k]
        for slot in (3, 2, 1):
            index = at + 4 * k + slot
            copy = push(
                gram_own.at[k, quarter_of(others[slot])], gram_in.at[slot, k], send.at[index],
                recv.at[index], {"dp": peers[slot]},
            )
            copy.start()
            gram_sends.append(copy)
    at = sems(12)
    at_sib = sems(4)
    gram_out = []
    for k in range(3):
        for copy in gram_sends[3 * k : 3 * k + 3]:
            copy.wait_recv()
        gram_all[core, chip, k] = (
            gram_own[k, quarter_of(chip)] + gram_in[1, k] + (gram_in[2, k] + gram_in[3, k])
        )
        for slot in (3, 2, 1):
            area = gram_all.at[core, chip, k]
            index = at + 4 * k + slot
            copy = push(area, area, send.at[index], recv.at[index], {"dp": peers[slot]})
            copy.start()
            gram_out.append(copy)

    def gram_copy(side, slot):
        area = gram_all.at[side, others[slot]]
        index = at_sib + slot
        return push(area, area, send.at[index], recv.at[index], to_sib)

    gram_on = [gram_copy(core, slot) for slot in range(4)]
    gram_on[0].start()
    for slot in (1, 2, 3):
        for k in range(3):
            area = gram_all.at[core, others[slot], k]
            index = at + 4 * k + slot
            push(area, area, send.at[index], recv.at[index], {"dp": peers[slot]}).wait_recv()
        gram_on[slot].start()
    for slot in range(4):
        gram_copy(1 - core, slot).wait_recv()

    every = [
        jnp.concatenate([gram_all[index // 3, item, index % 3] for item in range(4)], axis=0)
        for index in range(6)
    ]
    row_id = lax.broadcasted_iota(jnp.int32, (tile, tile), 0)
    col_id = lax.broadcasted_iota(jnp.int32, (tile, tile), 1)
    diagonal = jnp.where(row_id == col_id, every[0] + every[3] + every[5], 0.0)
    trace = jnp.sum(jnp.sum(diagonal, axis=1, keepdims=True), axis=0, keepdims=True)
    scale = 1.0 / (jnp.sqrt(trace) + 1e-07)

    value = iterate[...] * scale
    iterate[...] = value
    iter_up[...] = value.astype(bf16)
    def block(i, j):
        return slice(i * tile, (i + 1) * tile), slice(j * tile, (j + 1) * tile)

    def mirror(ref, column, values):
        ref[: (column + 1) * tile, block(0, column)[1]] = values
        for i in range(column):
            ref[block(column, i)] = values[i * tile : (i + 1) * tile].T

    def mirror_pair(pair, column, values):
        for ref, part in zip(pair, split_pair(values)):
            mirror(ref, column, part)

    def left_rows(pair, column):
        upper, lower = (ref[: (column + 1) * tile] for ref in pair)
        return jnp.concatenate([upper, upper, lower], axis=1)

    def right_columns(pair, column):
        upper, lower = (ref[:, block(0, column)[1]] for ref in pair)
        return jnp.concatenate([upper, lower, upper], axis=0)

    gram_pair, poly_pair, half_pair = (gram_up, gram_low), (poly_up, poly_low), (half_up, half_low)
    for index, (i, j) in enumerate(pairs):
        gram[block(i, j)] = every[index] * (scale * scale)
    for column in range(3):
        mirror_pair(gram_pair, column, gram[: (column + 1) * tile, block(0, column)[1]])
    each_plane(lambda plane: sums_chain.hop(plane, 0, 2))
    update_chain = Chain(update_ref, sizes, send, recv, sems)

    for sweep in range(ITERS):
        first, last = sweep == 0, sweep == ITERS - 1
        for column in range(3):
            rows, lanes = slice(0, (column + 1) * tile), block(0, column)[1]
            if first:
                square = dot_nn(left_rows(gram_pair, column), right_columns(gram_pair, column))
            else:
                square = dot_nn(gram_up[rows], gram_up[:, lanes])
            values = POLY_SECOND * gram[rows, lanes] + POLY_THIRD * square
            if first:
                mirror_pair(poly_pair, column, values)
            else:
                mirror(poly_up, column, values.astype(bf16))

        if last:
            part = units // 3
            for index in range(3):
                rows = slice(index * part, (index + 1) * part)
                values = POLY_FIRST * iterate[rows] + dot_nn(iter_up[rows], poly_up[...])
                update_ref[z, rows] = values.astype(bf16)
                each_plane(
                    lambda plane: [update_chain.start(plane, 2 * index + i) for i in range(2)]
                )
            continue

        for column in range(3):
            rows, lanes = slice(0, (column + 1) * tile), block(0, column)[1]
            if first:
                update = dot_nn(left_rows(poly_pair, column), right_columns(gram_pair, column))
            else:
                update = dot_nn(poly_up[rows], gram_up[:, lanes])
            values = POLY_FIRST * gram[rows, lanes] + update
            half[rows, lanes] = values
            if first:
                mirror_pair(half_pair, column, values)
            else:
                mirror(half_up, column, values.astype(bf16))

        for column in range(3):
            rows, lanes = slice(0, (column + 1) * tile), block(0, column)[1]
            if first:
                update = dot_nn(left_rows(half_pair, column), right_columns(poly_pair, column))
            else:
                update = dot_nn(half_up[rows], poly_up[:, lanes])
            values = POLY_FIRST * half[rows, lanes] + update
            gram[rows, lanes] = values
            mirror(gram_up, column, values.astype(bf16))

        values = POLY_FIRST * iterate[...] + dot_nn(iter_up[...], poly_up[...])
        iterate[...] = values
        iter_up[...] = values.astype(bf16)
        if sweep == 1:
            each_plane(lambda plane: sums_chain.hop(plane, 2, 3))
        elif sweep == 3:
            each_plane(lambda plane: sums_chain.hop(plane, 3, 4))

    def last_exchange(plane):
        update_chain.hop(plane, 0, 4)
        sums_chain.finish(plane)
        update_chain.finish(plane)

    each_plane(last_exchange)
    for copy in back_in:
        copy.wait_recv()
    for copy in back_out + gram_sends + gram_out + gram_on + gram_sib:
        copy.wait_send()


def muon(own, totals, centers, grad, moms, sizes):
    units, width = own.shape
    tile = width // 3
    low_rows = pltpu.VMEM((units, width), bf16)
    rows_f32 = pltpu.VMEM((units, width), f32)
    square_f32 = pltpu.VMEM((width, width), f32)
    square_low = pltpu.VMEM((width, width), bf16)
    blocks = pltpu.VMEM((3, tile, tile), f32)
    every = jax.ShapeDtypeStruct((4, units, width), bf16)
    return pl.pallas_call(
        functools.partial(muon_kernel, sizes),
        out_shape=(every, every, jax.ShapeDtypeStruct(grad.shape, bf16)),
        in_specs=[HBM_SPEC] * 4 + [ANY_SPEC] * 4,
        out_specs=(VMEM_SPEC,) * 3,
        scratch_shapes=[
            pltpu.VMEM(totals.shape, f32),
            pltpu.VMEM(centers.shape, f32),
            pltpu.SemaphoreType.DMA((4,)),
            blocks, blocks, blocks,
            pltpu.VMEM((4, 3, tile // 4, tile), f32),
            pltpu.VMEM((2, 4, 3, tile // 4, tile), f32),
            square_f32, square_low, square_low, square_low, square_low,
            square_f32, square_low, square_low,
            rows_f32, low_rows, low_rows,
            pltpu.VMEM(moms[3].shape, f32), rows_f32,
            pltpu.SemaphoreType.DMA((4,)),
            pltpu.SemaphoreType.DMA((168,)),
            pltpu.SemaphoreType.DMA((168,)),
        ],
        compiler_params=pltpu.CompilerParams(
            collective_id=1, has_side_effects=True, vmem_limit_bytes=VMEM_MUON
        ),
        name="muon",
    )(
        *[pltpu.with_memory_space_constraint(a, pltpu.HBM) for a in (own, totals, centers, grad)],
        *moms,
    )


def finish_kernel(
    sums_ref, updates_ref, total_ref, centers_ref, vec_ref, grad_ref, *rest
):
    tokens_ref, rest = rest[0], rest[1:]
    mom_refs, w_refs, mom_outs, w_outs, copy_outs = (rest[4 * i : 4 * i + 4] for i in range(5))
    grad_out_ref, vec_total_ref, vec_new_ref, tokens_out_ref = rest[20:24]
    mom_bufs, w_bufs, low_bufs = (rest[24 + 4 * i : 28 + 4 * i] for i in range(3))
    sems = rest[36]
    units = updates_ref.shape[1]
    dp, core, chip, _, _, _ = place()

    def by_core(row):
        return jnp.where(core == 0, row[:, :units], row[:, units:])

    own_total = total_ref[pl.ds(16 + dp, 1), :]
    sizes = (units, w_refs[1].shape[0], w_refs[2].shape[0], units)
    sums = (
        None,
        own_total[:, : sizes[1]],
        own_total[:, units : units + sizes[2]],
        by_core(total_ref[pl.ds(7 + chip, 1), :]),
    )
    rates = (
        RATE_PROJ * math.sqrt(FF / D), RATE_QKV * math.sqrt(QKV / D), RATE_OUT,
        RATE_FC * math.sqrt(FF / D),
    )
    centers = (None, centers_ref[2:3], centers_ref[3:4], centers_ref[0:1])
    stores = [pltpu.make_async_copy(tokens_ref, tokens_out_ref, sems.at[20])]
    stores[0].start()

    def leave(source, target, index):
        copy = pltpu.make_async_copy(source, target, sems.at[index])
        copy.start()
        stores.append(copy)

    for i in range(4):
        if i == 0:
            spike = dot_tn(row_repeat(centers_ref[1:2, :units]), row_splits(total_ref[14:15]))
            total = sums_ref[i].astype(f32) + spike
        elif i < 3:
            spike = dot_tn(row_splits(sums[i]), row_repeat(centers[i]))
            total = sums_ref[i, : sizes[i]].astype(f32) + spike
        else:
            spike = dot_tn(row_repeat(centers[i]), row_splits(sums[i]))
            total = sums_ref[i].astype(f32).T + spike
        mom_bufs[i][...] = MOMENT_DECAY * mom_refs[i][...] + total
        leave(mom_bufs[i], mom_outs[i], 8 + i)
        update = updates_ref[i, : sizes[i]].astype(f32)
        if i == 3:
            update = update.T
        new = w_refs[i][...] - rates[i] * update
        w_bufs[i][...] = new
        leave(w_bufs[i], w_outs[i], 12 + i)
        low_bufs[i][...] = new.astype(bf16)
        leave(low_bufs[i], copy_outs[i], 16 + i)

    grad_out_ref[...] = grad_ref[...].astype(f32)
    vec_total = total_ref[: vec_ref.shape[0]]
    vec_total_ref[...] = vec_total
    vec_new_ref[...] = vec_ref[...] - RATE_VEC * vec_total * lax.rsqrt(
        jnp.mean(vec_total * vec_total, axis=-1, keepdims=True) + NORM_EPS
    )
    for copy in stores:
        copy.wait()


def finish(sums, updates, totals, centers, vectors, grad, tokens, moms, weights):
    full = [jax.ShapeDtypeStruct(w.shape, f32) for w in weights]
    low = [jax.ShapeDtypeStruct(w.shape, bf16) for w in weights]
    return pl.pallas_call(
        finish_kernel,
        out_shape=(
            *full, *full, *low,
            jax.ShapeDtypeStruct(grad.shape, f32),
            jax.ShapeDtypeStruct(vectors.shape, f32),
            jax.ShapeDtypeStruct(vectors.shape, f32),
            jax.ShapeDtypeStruct(tokens.shape, bf16),
        ),
        in_specs=[VMEM_SPEC] * 6 + [ANY_SPEC] + [VMEM_SPEC] * 8,
        out_specs=(ANY_SPEC,) * 12 + (VMEM_SPEC,) * 3 + (ANY_SPEC,),
        scratch_shapes=[
            *[pltpu.VMEM(w.shape, f32) for w in weights],
            *[pltpu.VMEM(w.shape, f32) for w in weights],
            *[pltpu.VMEM(w.shape, bf16) for w in weights],
            pltpu.SemaphoreType.DMA((21,)),
        ],
        compiler_params=pltpu.CompilerParams(vmem_limit_bytes=VMEM_FINISH),
        name="finish",
    )(sums, updates, totals, centers, vectors, grad, tokens, *moms, *weights)


def per_device_any(
    inputs, teacher, counts, groups, group_weight, w_qkv, w_out, w_fc, w_proj,
    vectors, mom_qkv, mom_out, mom_fc, mom_proj,
):
    width = inputs.shape[-1]
    z = lax.axis_index("blk")
    dp = lax.axis_index("dp")

    low_qkv = w_qkv.T.astype(bf16)
    low_out = w_out.T.astype(bf16)
    low_fc = w_fc.T.astype(bf16)
    low_proj = w_proj.astype(bf16)
    full_qkv = lax.all_gather(low_qkv, "dp", axis=0, tiled=True)
    full_out = lax.all_gather(low_out, "dp", axis=0, tiled=True)

    x = lax.all_to_all(inputs, "blk", 0, 1, tiled=True)[0].astype(f32)
    target_in = lax.all_to_all(teacher, "blk", 0, 1, tiled=True)[0].astype(f32)
    length = x.shape[0]
    chosen = (groups[z] == jnp.arange(GROUPS, dtype=jnp.int32)).astype(f32)
    seq_weight = jnp.sum(chosen * group_weight) * (z < counts[0]).astype(f32)

    unit_one, scale_one = norm_parts(x)
    normed = (unit_one * vectors[0] + vectors[1]).astype(bf16)
    mixed = dot_nt(normed, full_qkv)
    queries = (mixed[:, :width] + vectors[2]).astype(bf16)
    keys = mixed[:, width : 2 * width].astype(bf16)
    values = (mixed[:, 2 * width :] + vectors[3]).astype(bf16)

    def heads(a):
        return a.reshape(length, H, HD).transpose(1, 0, 2)

    def flat(a):
        return a.transpose(1, 0, 2).reshape(length, width)

    q_h, k_h, v_h = heads(queries), heads(keys), heads(values)
    pos = jnp.arange(length, dtype=jnp.int32)
    visible = pos[None, :] <= pos[:, None]
    scores = jnp.einsum("hqd,hkd->hqk", q_h, k_h, preferred_element_type=f32) * 0.125
    scores = jnp.where(visible, scores, MASKED)
    peak = jnp.max(scores, axis=-1, keepdims=True)
    weights = jnp.exp(scores - peak)
    probs = weights / jnp.sum(weights, axis=-1, keepdims=True)
    probs_low = probs.astype(bf16)
    att_h = jnp.einsum("hqk,hkd->hqd", probs_low, v_h, preferred_element_type=f32)
    attended_low = flat(att_h).astype(bf16)
    hidden = x + dot_nt(attended_low, full_out) + vectors[4]
    unit_two, scale_two = norm_parts(hidden)
    normed_two = (unit_two * vectors[5] + vectors[6]).astype(bf16)

    token_total = length * lax.axis_size("dp") * lax.axis_size("blk")
    means = lax.psum(
        jnp.stack(
            [jnp.sum(rows.astype(f32), axis=0) for rows in (normed, attended_low, normed_two)]
        ),
        ("dp", "blk"),
    ) / token_total
    all_two = lax.all_gather(normed_two, "dp", axis=0, tiled=True)
    hidden_units = low_fc.shape[0]
    fc_rows = FF // D
    fc_bias = lax.dynamic_slice(
        vectors[7 : 7 + fc_rows].reshape(FF), (dp * hidden_units,), (hidden_units,)
    )
    gate_in = dot_nt(all_two, low_fc) + fc_bias
    active, slope = gelu_both(gate_in)
    active_low = active.astype(bf16)
    active_mean = lax.psum(jnp.sum(active_low.astype(f32), axis=0), "blk") / token_total
    part_out = dot_nn(active_low, low_proj).astype(bf16)
    block_out = (
        hidden
        + lax.psum_scatter(part_out, "dp", scatter_dimension=0, tiled=True).astype(f32)
        + vectors[7 + fc_rows]
    )
    student = jax.nn.softmax(block_out / TEMPER, axis=-1)
    target = jax.nn.softmax(target_in / TEMPER, axis=-1)
    grad_y = (seq_weight * (width / TEMPER)) * (student - target)
    grad_y_low = grad_y.astype(bf16)
    all_grad_y = lax.all_gather(grad_y_low, "dp", axis=0, tiled=True)
    grad_gate = (dot_nt(all_grad_y, low_proj) * slope).astype(bf16)
    part_two = dot_nn(grad_gate, low_fc).astype(bf16)
    grad_normed_two = lax.psum_scatter(
        part_two, "dp", scatter_dimension=0, tiled=True
    ).astype(f32)
    grad_fc_bias = jnp.sum(grad_gate.astype(f32), axis=0)
    sum_grad_y = jnp.sum(all_grad_y.astype(f32), axis=0)
    grad_proj = dot_tn(active_low, all_grad_y) - active_mean[:, None] * sum_grad_y
    grad_fc = dot_tn(grad_gate, all_two) - grad_fc_bias[:, None] * means[2]

    back_two, grad_gain_two, grad_bias_two = norm_back(
        unit_two, scale_two, vectors[5], grad_normed_two
    )
    grad_hidden = grad_y + back_two
    grad_hidden_low = grad_hidden.astype(bf16)
    sum_grad_hidden = jnp.sum(grad_hidden_low.astype(f32), axis=0)
    grad_out = dot_tn(grad_hidden_low, attended_low) - sum_grad_hidden[:, None] * means[1]
    grad_att = dot_nn(grad_hidden_low, full_out).astype(bf16)
    ga_h = heads(grad_att)
    delta = jnp.sum(ga_h.astype(f32) * att_h, axis=-1, keepdims=True)
    grad_probs = jnp.einsum("hqd,hkd->hqk", ga_h, v_h, preferred_element_type=f32)
    grad_scores = (probs * (grad_probs - delta)).astype(bf16)
    grad_q = jnp.einsum("hqk,hkd->hqd", grad_scores, k_h, preferred_element_type=f32) * 0.125
    grad_k = jnp.einsum("hqk,hqd->hkd", grad_scores, q_h, preferred_element_type=f32) * 0.125
    grad_v = jnp.einsum("hqk,hqd->hkd", probs_low, ga_h, preferred_element_type=f32)
    grad_mixed = jnp.concatenate([flat(grad_q), flat(grad_k), flat(grad_v)], axis=-1).astype(bf16)
    bias_sums = jnp.sum(grad_mixed.astype(f32), axis=0)
    grad_qkv = dot_tn(grad_mixed, normed) - bias_sums[:, None] * means[0]
    back_one, grad_gain_one, grad_bias_one = norm_back(
        unit_one, scale_one, vectors[0], dot_nn(grad_mixed, full_qkv)
    )
    grad_input = grad_hidden + back_one

    sum_qkv = lax.psum_scatter(grad_qkv.astype(bf16), "dp", scatter_dimension=0, tiled=True)
    sum_out = lax.psum_scatter(grad_out.astype(bf16), "dp", scatter_dimension=0, tiled=True)
    shard_sums = lax.psum(
        jnp.concatenate([sum_qkv, sum_out, grad_fc.astype(bf16), grad_proj.astype(bf16)]), "blk"
    ).astype(f32)
    vec_grad = jnp.concatenate(
        [
            jnp.stack(
                [
                    grad_gain_one, grad_bias_one, bias_sums[:width], bias_sums[2 * width :],
                    jnp.sum(grad_hidden, axis=0), grad_gain_two, grad_bias_two,
                ]
            ),
            lax.dynamic_update_slice(
                jnp.zeros((FF,), f32), grad_fc_bias, (dp * hidden_units,)
            ).reshape(fc_rows, width),
            jnp.stack(
                [
                    jnp.sum(grad_y, axis=0), bias_sums[width : 2 * width], sum_grad_hidden,
                    jnp.sum(grad_y_low.astype(f32), axis=0),
                ]
            ),
        ],
        axis=0,
    )
    vec_all = lax.psum(vec_grad, ("dp", "blk"))
    vec_total = vec_all[: vectors.shape[0]]
    sums_qkv = jnp.concatenate([vec_all[2], vec_all[12], vec_all[3]])

    n_qkv, n_out, n_fc = w_qkv.shape[1], w_out.shape[1], w_fc.shape[1]
    cuts = (0, n_qkv, n_qkv + n_out, n_qkv + n_out + n_fc, n_qkv + n_out + 2 * n_fc)
    def own(sums, count):
        return lax.dynamic_slice(sums, (dp * count,), (count,))[:, None]

    spikes = (
        own(sums_qkv, n_qkv) * means[0],
        own(vec_all[13], n_out) * means[1],
        own(vec_all[7 : 7 + fc_rows].reshape(FF), n_fc) * means[2],
        active_mean[:, None] * vec_all[14],
    )
    new_moms = [
        MOMENT_DECAY * mom + (shard_sums[low:high] + spike)
        for mom, low, high, spike in zip(
            (mom_qkv.T, mom_out.T, mom_fc.T, mom_proj), cuts[:-1], cuts[1:], spikes
        )
    ]
    stacked = jnp.stack(
        [jnp.pad(mom, ((0, n_fc - mom.shape[0]), (0, 0))) for mom in new_moms]
    )
    rows = lax.dynamic_index_in_dim(stacked, z, 0, keepdims=False)
    gram = lax.psum(three_pass(dot_tn, rows, rows), "dp")
    rows = newton_schulz(rows, gram)
    updates = lax.all_gather(rows.astype(bf16), "blk", axis=0).astype(f32)
    qkv_new = w_qkv - RATE_QKV * math.sqrt(QKV / D) * updates[0, :n_qkv].T
    out_new = w_out - RATE_OUT * updates[1, :n_out].T
    fc_new = w_fc - RATE_FC * math.sqrt(FF / D) * updates[2].T
    proj_new = w_proj - RATE_PROJ * math.sqrt(FF / D) * updates[3]
    vectors_new = vectors - RATE_VEC * vec_total * lax.rsqrt(
        jnp.mean(vec_total * vec_total, axis=-1, keepdims=True) + NORM_EPS
    )
    outputs = lax.all_to_all(block_out.astype(bf16)[None], "blk", 1, 0, tiled=True)
    input_grad = lax.all_to_all(grad_input.astype(bf16)[None], "blk", 1, 0, tiled=True)
    return (
        outputs,
        input_grad.astype(f32),
        new_moms[0].T,
        new_moms[1].T,
        new_moms[2].T,
        new_moms[3],
        qkv_new,
        out_new,
        fc_new,
        proj_new,
        qkv_new.astype(bf16),
        out_new.astype(bf16),
        fc_new.astype(bf16),
        proj_new.astype(bf16),
        vec_total,
        vectors_new,
    )


def per_device(
    inputs, teacher, counts, groups, group_weight, w_qkv, w_out, w_fc, w_proj,
    vectors, mom_qkv, mom_out, mom_fc, mom_proj,
):
    sizes = (w_fc.shape[1], w_qkv.shape[1], w_out.shape[1], w_proj.shape[0])
    outputs, grad, own, totals, centers = token_pass(
        counts, groups, group_weight, inputs, teacher, w_qkv.T, w_out.T, w_fc, w_proj, vectors
    )
    moms = (mom_proj, mom_qkv.T, mom_out.T, mom_fc)
    sums, updates, grads = muon(own, totals, centers, grad, moms, sizes)
    done = finish(
        sums, updates, totals, centers, vectors, grads, outputs, moms, (w_proj, w_qkv.T, w_out.T, w_fc)
    )

    def ordered(start):
        return (done[start + 1].T, done[start + 2].T, done[start + 3], done[start])

    return (done[15], done[12], *ordered(0), *ordered(4), *ordered(8), done[13], done[14])


def solution(mesh):
    token = P("dp", "blk", None)
    column = P(None, "dp")
    row = P("dp", None)
    in_specs = (
        token, token, P("dp"), P("dp"), P(), column, column, column, row, P(),
        column, column, column, row,
    )
    out_specs = (
        token, token, column, column, column, row, column, column, column, row,
        column, column, column, row, P(), P(),
    )
    body = per_device if dict(mesh.shape) == {"dp": 8, "blk": 4} else per_device_any
    return jax.shard_map(
        body, mesh=mesh, in_specs=in_specs, out_specs=out_specs, check_vma=False
    )
```
